32 devices in a mesh: seq: 8 (over z, x), head: 4 (over y, core).
Axes of the slice: x: 2, y: 2, z: 4, core: 2. Of those that a mesh axis runs over, the one named last changes fastest.
Arguments:
- query_in: bfloat16 [4096, 256], P('seq', 'head'), may hold values from -6 to 6
- key_in: bfloat16 [4096, 256], P('seq', 'head'), may hold values from -6 to 6
- value_in: bfloat16 [4096, 2048], P('seq', 'head'), may hold values from -8 to 8
- conv_query: float32 [3, 256], P(None, 'head'), may hold values from -3.5 to 3.5
- conv_key: float32 [3, 256], P(None, 'head'), may hold values from -3.5 to 3.5
- conv_value: float32 [3, 2048], P(None, 'head'), may hold values from -3.5 to 3.5
- out_proj: bfloat16 [2048, 2048], P('head'), may hold values from -0.125 to 0.125
- out_grad: bfloat16 [4096, 2048], P(('seq', 'head')), may hold values from -8 to 8
Outputs:
- mixed: bfloat16 [4096, 2048], P(('seq', 'head'))
- grad_query: float32 [4096, 256], P('seq', 'head')
- grad_key: float32 [4096, 256], P('seq', 'head')
- grad_value: float32 [4096, 2048], P('seq', 'head')
- grad_conv_query: float32 [3, 256], P(None, 'head')
- grad_conv_key: float32 [3, 256], P(None, 'head')
- grad_conv_value: float32 [3, 2048], P(None, 'head')
The draws below stay inside these ranges and needn't reach their ends.
All inputs are finite; a program needn't handle non-finite values.
Results may differ from the reference program's by a relative error of at most 0.0049.
Values may be sent and summed in bfloat16 or wider, within the bound.
A program may use at most 192 MiB of HBM per device.

```python
import math
import jax
import jax.numpy as jnp
import numpy as np
from jax import lax

D = 2048
HEADS = 16
FK = 16
VD = 128
FEAT = 153
TOKENS = 4096


def offset_field(key, row_count, col_count):
    subkeys = jax.random.split(key, 3)
    channel_mean = jax.random.normal(subkeys[0], (1, col_count), jnp.float32)
    offsets = jax.random.normal(subkeys[1], (row_count // 64, 1, col_count), jnp.float32)
    jitter = jax.random.normal(subkeys[2], (row_count // 64, 64, col_count), jnp.float32)
    values_all = (jitter + offsets).reshape(row_count, col_count) + channel_mean
    return jnp.clip(values_all, -8.0, 8.0)


def draw_value_in(key, part):
    return offset_field(jax.random.fold_in(key, 3), TOKENS, HEADS * VD).astype(jnp.bfloat16)


def draw_out_grad(key, part):
    return offset_field(jax.random.fold_in(key, 5), TOKENS, D).astype(jnp.bfloat16)


def block_levels(stream_key, dims, pieces, low, top_value):
    loudness, own = 1.0, jax.random.fold_in(stream_key, 6)
    for position, blocks in pieces:
        steps = jnp.exp(jax.random.uniform(jax.random.fold_in(own, position), (blocks,), jnp.float32, low / len(pieces), top_value / len(pieces)))
        loudness = loudness * jnp.repeat(steps, dims[position] // blocks).reshape([-1 if axis == position else 1 for axis in range(len(dims))])
    return loudness


def gaussian(rng, shape, scale, bound, shards=(), held_as=jnp.bfloat16):
    loudness = block_levels(rng, shape, shards, -0.22, 0.18) if shards else 1.0
    result = jax.random.normal(rng, shape, jnp.float32) * scale * loudness
    return jnp.minimum(jnp.maximum(result, -bound), bound).astype(held_as)


def setup_inputs(seed: int = 0) -> dict:
    seeds = jax.random.split(jax.random.key(seed), 9)
    return {
        "query_in": gaussian(seeds[0], (TOKENS, HEADS * FK), 1.0, 6.0, ((0, 8), (1, 4))),
        "key_in": gaussian(seeds[1], (TOKENS, HEADS * FK), 1.0, 6.0, ((0, 8), (1, 4))),
        "value_in": draw_value_in(jax.random.fold_in(seeds[8], 71), 0),
        "conv_query": gaussian(seeds[3], (3, HEADS * FK), 3 ** -0.5, 3.5, ((1, 4),), jnp.float32),
        "conv_key": gaussian(seeds[4], (3, HEADS * FK), 3 ** -0.5, 3.5, ((1, 4),), jnp.float32),
        "conv_value": gaussian(seeds[5], (3, HEADS * VD), 3 ** -0.5, 3.5, ((1, 4),), jnp.float32),
        "out_proj": gaussian(seeds[6], (HEADS * VD, D), (HEADS * VD) ** -0.5, 0.125, ((0, 4),)),
        "out_grad": draw_out_grad(jax.random.fold_in(seeds[8], 71), 0),
    }


HIGHEST = lax.Precision.HIGHEST

def pair_table(feature_dim):
    mapping = np.zeros((feature_dim * feature_dim, feature_dim * (feature_dim + 1) // 2), np.float32)
    column = 0
    for row_index in range(feature_dim):
        for col_index in range(row_index, feature_dim):
            if row_index == col_index:
                mapping[row_index * feature_dim + col_index, column] = 1.0 / math.sqrt(2.0 * feature_dim)
            else:
                mapping[row_index * feature_dim + col_index, column] = 1.0 / math.sqrt(feature_dim)
            column = column + 1
    return mapping

def features(inputs):
    feature_dim = inputs.shape[-1]
    linear = inputs * feature_dim ** (-0.25)
    products = (inputs[..., :, None] * inputs[..., None, :]).reshape(inputs.shape[:-1] + (feature_dim * feature_dim,))
    quadratic = jnp.dot(products, jnp.asarray(pair_table(feature_dim)).astype(inputs.dtype), precision=HIGHEST)
    constant = jnp.ones(inputs.shape[:-1] + (1,), inputs.dtype)
    return jnp.concatenate([constant, linear, quadratic], axis=-1)

def causal_conv(extended, weights, length):
    total = weights[0] * extended[2:length + 2]
    total = total + weights[1] * extended[1:length + 1]
    return total + weights[2] * extended[0:length]

def padded(inputs):
    return jnp.concatenate([jnp.zeros((2, inputs.shape[1]), jnp.float32), inputs], axis=0)

def attention_step(carry, block_inputs):
    state, norm_sum = carry
    query_blk, key_blk, value_blk = block_inputs
    phi_query = features(query_blk)
    phi_key = features(key_blk)
    block_len = query_blk.shape[0]
    causal = (lax.broadcasted_iota(jnp.int32, (block_len, block_len), 0) >= lax.broadcasted_iota(jnp.int32, (block_len, block_len), 1)).astype(jnp.float32)
    similarity = jnp.einsum('thf,shf->hts', query_blk, key_blk, precision=HIGHEST) * FK ** (-0.5)
    weights = (1.0 + similarity + 0.5 * similarity * similarity) * causal
    numerator = jnp.einsum('hts,shv->thv', weights, value_blk, precision=HIGHEST) + jnp.einsum('thf,hfv->thv', phi_query, state, precision=HIGHEST)
    denominator = lax.optimization_barrier(jnp.sum(weights, axis=2)).T + jnp.einsum('thf,hf->th', phi_query, norm_sum, precision=HIGHEST)
    state = state + jnp.einsum('shf,shv->hfv', phi_key, value_blk, precision=HIGHEST)
    norm_sum = norm_sum + lax.optimization_barrier(jnp.sum(phi_key, axis=0))
    return ((state, norm_sum), numerator / denominator[:, :, None])

def mixer(query_f, key_f, value_f, conv_query, conv_key, conv_value):
    length = query_f.shape[0]
    query_conv = causal_conv(padded(query_f), conv_query, length)
    key_conv = causal_conv(padded(key_f), conv_key, length)
    value_conv = causal_conv(padded(value_f), conv_value, length)
    block_rows = math.gcd(length, 512)
    block_count = length // block_rows
    query_blocks = query_conv.reshape(block_count, block_rows, HEADS, FK)
    key_blocks = key_conv.reshape(block_count, block_rows, HEADS, FK)
    value_blocks = value_conv.reshape(block_count, block_rows, HEADS, VD)
    start_state = (jnp.zeros((HEADS, FEAT, VD), jnp.float32), jnp.zeros((HEADS, FEAT), jnp.float32))
    final_carry, outputs = lax.scan(jax.checkpoint(attention_step), start_state, (query_blocks, key_blocks, value_blocks))
    return outputs.reshape(length, HEADS, VD)

def reference(query_in, key_in, value_in, conv_query, conv_key, conv_value, out_proj, out_grad):
    attended, pullback = jax.vjp(mixer, query_in.astype(jnp.float32), key_in.astype(jnp.float32), value_in.astype(jnp.float32), conv_query, conv_key, conv_value)
    length = attended.shape[0]
    flat_attended = attended.reshape(length, HEADS * VD).astype(jnp.bfloat16)
    mixed = jnp.dot(flat_attended, out_proj, preferred_element_type=jnp.float32).astype(jnp.bfloat16)
    upstream = jnp.dot(out_grad, out_proj.T, preferred_element_type=jnp.float32).reshape(length, HEADS, VD)
    grads = pullback(upstream)
    return (mixed, grads[0], grads[1], grads[2], grads[3], grads[4], grads[5])
```

```python
import functools
import math

import jax
import jax.numpy as jnp
import ml_dtypes
import numpy as np
from jax import lax
from jax.experimental import pallas as pl
from jax.experimental.pallas import tpu as pltpu
from jax.sharding import PartitionSpec as P

VD = 128
LANES = 128
RIM = 8
MESH = pl.DeviceIdType.MESH
F32, BF16 = jnp.float32, jnp.bfloat16
NN = (((1,), (0,)), ((), ()))
NT = (((1,), (1,)), ((), ()))
TN = (((0,), (0,)), ((), ()))


def round_up(number, step):
    return (number + step - 1) // step * step


def feature_tables(fk, heads):
    feat = fk * (fk + 1) // 2 + fk + 1
    lanes = round_up(feat, LANES)
    pick_a = np.zeros((heads, heads * fk, lanes), np.float32)
    pick_b = np.zeros((heads, heads * fk, lanes), np.float32)
    rows = np.zeros((8, lanes), np.float32)
    column = 0
    for i in range(fk):
        for j in range(i, fk):
            for h in range(heads):
                pick_a[h, h * fk + i, column] = 1.0
                pick_b[h, h * fk + j, column] = 1.0
            rows[2, column] = 1.0 / math.sqrt(2.0 * fk if i == j else fk)
            column += 1
    for i in range(fk):
        for h in range(heads):
            pick_a[h, h * fk + i, column] = 1.0
        rows[1, column] = 1.0
        rows[2, column] = fk ** -0.25
        column += 1
    rows[0, column] = rows[1, column] = rows[2, column] = 1.0
    mask = np.zeros((heads, 8, heads * fk), np.float32)
    for h in range(heads):
        mask[h, :, h * fk : (h + 1) * fk] = 1.0
    return pick_a.astype(ml_dtypes.bfloat16), pick_b.astype(ml_dtypes.bfloat16), rows, mask, feat


def dot(a, b, dims):
    return lax.dot_general(a, b, dims, preferred_element_type=F32)


def split(x):
    high = x.astype(BF16)
    return high, (x - high.astype(F32)).astype(BF16)


def dot3(a, b, dims):
    return dot(a[0], b[0], dims) + dot(a[0], b[1], dims) + dot(a[1], b[0], dims)


def kernel(n_seq, n_head, fk, feat_rows,
           q_ref, k_ref, v_ref, cq_ref, ck_ref, cv_ref, w_ref, og_ref,
           pa_ref, pb_ref, rows_ref, mask_ref,
           mixed_ref, gq_ref, gk_ref, gv_ref, gcq_ref, gck_ref, gcv_ref,
           ext, gcon, qs, ks, vs, pq, pk, dsim, wh, wl, num, den, up, dgr, att, gvs,
           og_all, m_send, m_recv, m_own,
           tf, rf, pf, tb, rb, pb, tt, tr,
           halo_sem, og_sem, m_sem, f_sem, b_sem, t_sem):
    T, HK = q_ref.shape
    VC = v_ref.shape[1]
    H = VC // VD
    CW = ext.shape[1]
    FP = feat_rows
    FL = pa_ref.shape[2]
    TS = T // n_head
    bits = [1 << i for i in range(n_seq.bit_length() - 1)]
    L = len(bits)
    s = lax.axis_index("seq")
    h_me = lax.axis_index("head")

    def flip(index, b):
        return index + b - 2 * b * ((index // b) % 2)

    def flip_all(index, r):
        b = 1
        while b <= r:
            if r & b:
                index = flip(index, b)
            b *= 2
        return index

    nxt = (s + 1) % n_seq
    prv = (s + n_seq - 1) % n_seq

    barrier = pltpu.get_barrier_semaphore()
    for b in bits:
        pl.semaphore_signal(barrier, inc=1, device_id={"seq": flip(s, b)}, device_id_type=MESH)
    for other in (nxt, prv):
        pl.semaphore_signal(barrier, inc=1, device_id={"seq": other}, device_id_type=MESH)
    for r in range(1, n_head):
        pl.semaphore_signal(barrier, inc=1, device_id={"head": flip_all(h_me, r)}, device_id_type=MESH)

    zero_pad = jnp.zeros((T, LANES - HK), F32)
    ext[RIM:, 0:LANES] = jnp.concatenate([q_ref[...].astype(F32), zero_pad], axis=1)
    ext[RIM:, LANES : 2 * LANES] = jnp.concatenate([k_ref[...].astype(F32), zero_pad], axis=1)
    ext[RIM:, 2 * LANES :] = v_ref[...].astype(F32)

    pl.semaphore_wait(barrier, L + 2 + n_head - 1)

    def remote(src, dst, sem, where):
        return pltpu.make_async_remote_copy(
            src_ref=src, dst_ref=dst, send_sem=sem[0], recv_sem=sem[1],
            device_id=where, device_id_type=MESH)

    halo = remote(ext.at[pl.ds(T, RIM)], ext.at[pl.ds(0, RIM)],
                  (halo_sem.at[0, 0], halo_sem.at[0, 1]), {"seq": nxt})
    halo.start()

    head_bits = [1 << i for i in reversed(range(n_head.bit_length() - 1))]
    og_copies = {}
    held = [0]
    for b in head_bits:
        for r in held:
            src = og_ref if r == 0 else og_all.at[r]
            og_copies[r ^ b] = (r, remote(src, og_all.at[r ^ b],
                                          (og_sem.at[r ^ b, 0], og_sem.at[r ^ b, 1]),
                                          {"head": flip(h_me, b)}))
        held = held + [r ^ b for r in held]
    for r, (src, copy) in og_copies.items():
        if src == 0:
            copy.start()

    def tap_row(j):
        pad = jnp.zeros((1, LANES - HK), F32)
        return jnp.concatenate(
            [cq_ref[j : j + 1, :], pad, ck_ref[j : j + 1, :], pad, cv_ref[j : j + 1, :]], axis=1)

    taps = [tap_row(j) for j in range(3)]

    halo.wait_recv()
    ext[0:RIM, :] = jnp.where(s == 0, 0.0, ext[0:RIM, :])

    def conv(lo, hi):
        total = taps[0][:, lo:hi] * ext[RIM : RIM + T, lo:hi]
        total = total + taps[1][:, lo:hi] * ext[RIM - 1 : RIM - 1 + T, lo:hi]
        return total + taps[2][:, lo:hi] * ext[RIM - 2 : RIM - 2 + T, lo:hi]

    qs[...] = conv(0, LANES)[:, :HK]
    ks[...] = conv(LANES, 2 * LANES)[:, :HK]
    for h in range(H):
        vs[h] = conv((2 + h) * LANES, (3 + h) * LANES)

    row_a = rows_ref[0:1, :]
    row_b = rows_ref[1:2, :]
    row_c = rows_ref[2:3, :]

    def factors(x, h):
        high, low = split(x)
        a = dot(high, pa_ref[h], NN) + dot(low, pa_ref[h], NN)
        b = dot(high, pb_ref[h], NN) + dot(low, pb_ref[h], NN)
        return (a + row_a) * row_c, b + row_b

    def pull(x, dphi, h):
        a, b = factors(x, h)
        left = split(dphi * b * row_c)
        right = split(dphi * a)
        return (dot(left[0], pa_ref[h], NT) + dot(left[1], pa_ref[h], NT)
                + dot(right[0], pb_ref[h], NT) + dot(right[1], pb_ref[h], NT))

    def put_state(buf, h, state, total):
        buf[0, h, 0:FP, :] = state
        for c in range(FL // LANES):
            buf[0, h, FP + c : FP + c + 1, :] = total[:, c * LANES : (c + 1) * LANES]

    def sums_of(buf, h):
        return jnp.concatenate(
            [buf[h, FP + c : FP + c + 1, :] for c in range(FL // LANES)], axis=1)

    def hop(send, recv, sem, l, h):
        return remote(send.at[l, h], recv.at[l, h], (sem.at[l, h, 0], sem.at[l, h, 1]),
                      {"seq": flip(s, bits[l])})

    def stage(send, recv, total, sem, l, later):
        bit = (s // bits[l]) % 2
        wanted = bit == (0 if later else 1)

        def one(h, _):
            hop(send, recv, sem, l, h).wait_recv()
            arrived = recv[l, h]
            mine = jnp.where(wanted, arrived, 0.0)
            total[h] = mine if l == 0 else total[h] + mine
            if l + 1 < L:
                send[l + 1, h] = send[l, h] + arrived
                hop(send, recv, sem, l + 1, h).start()
            return 0

        lax.fori_loop(0, H, one, 0)

    def key_side(h, _):
        a, b = factors(ks[...], h)
        phi = a * b
        pk[h] = phi
        state = dot3(split(phi[:, :FP]), split(vs[h]), TN)
        put_state(tf, h, state, jnp.sum(phi, axis=0, keepdims=True))
        hop(tf, rf, f_sem, 0, h).start()
        return 0

    for l in range(L):
        for h in range(H):
            for buf in (tf, tb):
                buf[l, h, FP:, :] = jnp.zeros((buf.shape[2] - FP, LANES), F32)
    lax.fori_loop(0, H, key_side, 0)

    def query_side(h, _):
        x = qs[...]
        a, b = factors(x, h)
        pq[h] = a * b
        sim = dot3(split(x * mask_ref[h, 0:1, :]), split(ks[...]), NT) * fk ** -0.5
        causal = (lax.broadcasted_iota(jnp.int32, (T, T), 0)
                  >= lax.broadcasted_iota(jnp.int32, (T, T), 1))
        weights = jnp.where(causal, 1.0 + sim + 0.5 * sim * sim, 0.0)
        dsim[h] = jnp.where(causal, (1.0 + sim) * fk ** -0.5, 0.0)
        high, low = split(weights)
        wh[h] = high
        wl[h] = low
        den[h] = jnp.sum(weights, axis=1, keepdims=True)
        return 0

    lax.fori_loop(0, H, query_side, 0)

    stage(tf, rf, pf, f_sem, 0, False)

    for r, (src, copy) in og_copies.items():
        if src != 0:
            og_copies[src][1].wait_recv()
            copy.start()

    def numer_side(h, _):
        num[h] = dot3((wh[h], wl[h]), split(vs[h]), NN)
        return 0

    lax.fori_loop(0, H, numer_side, 0)
    if L > 1:
        stage(tf, rf, pf, f_sem, 1, False)

    forwarded = {src for src, _ in og_copies.values() if src != 0}
    for r in held:
        if r != 0 and r not in forwarded:
            og_copies[r][1].wait_recv()
        block = og_ref[...] if r == 0 else og_all[r]
        first = pl.multiple_of(flip_all(h_me, r) * TS, TS)
        product = dot(block, w_ref[...], NT)
        for h in range(H):
            up[h, pl.ds(first, TS), :] = product[:, h * VD : (h + 1) * VD]

    for l in range(2, L):
        stage(tf, rf, pf, f_sem, l, False)

    def attend(h, _):
        phi = pq[h]
        denom = den[h] + jnp.sum(phi * sums_of(pf, h), axis=1, keepdims=True)
        phi_s = split(phi[:, :FP])
        numer = num[h] + dot3(phi_s, split(pf[h, 0:FP, :]), NN)
        inv = 1.0 / denom
        out = numer * inv
        att[h] = out.astype(BF16)
        upstream = up[h]
        g = upstream * inv
        up[h] = g
        dg = -jnp.sum(upstream * out, axis=1, keepdims=True) * inv
        dgr[h] = dg
        put_state(tb, h, dot3(phi_s, split(g), TN), jnp.sum(phi * dg, axis=0, keepdims=True))
        hop(tb, rb, b_sem, 0, h).start()
        return 0

    lax.fori_loop(0, H, attend, 0)

    def m_copy(r):
        return remote(m_send.at[r], m_recv.at[r], (m_sem.at[r, 0], m_sem.at[r, 1]),
                      {"head": flip_all(h_me, r)})

    for r in sorted(range(n_head), reverse=True):
        first = pl.multiple_of(flip_all(h_me, r) * TS, TS)
        block = jnp.concatenate([att[h, pl.ds(first, TS), :] for h in range(H)], axis=1)
        part = dot(block, w_ref[...], NN)
        if r:
            m_send[r] = part.astype(BF16)
            m_copy(r).start()
        else:
            m_own[...] = part

    stage(tb, rb, pb, b_sem, 0, True)

    gcon[0:T, 0 : 2 * LANES] = jnp.zeros((T, 2 * LANES), F32)

    def query_grads(h, _):
        g = split(up[h])
        dg = dgr[h]
        dphi = dot3(g, split(pf[h, 0:FP, :]), NT)
        dphi = jnp.concatenate([dphi, jnp.zeros((T, FL - FP), F32)], axis=1) + dg * sums_of(pf, h)
        ds = split((dot3(g, split(vs[h]), NT) + dg) * dsim[h])
        mask = mask_ref[h, 0:1, :]
        gcon[0:T, 0:HK] = (gcon[0:T, 0:HK] + pull(qs[...], dphi, h)
                           + dot3(ds, split(ks[...]), NN) * mask)
        gcon[0:T, LANES : LANES + HK] = (gcon[0:T, LANES : LANES + HK]
                                         + dot3(ds, split(qs[...]), TN) * mask)
        return 0

    lax.fori_loop(0, H, query_grads, 0)
    if L > 1:
        stage(tb, rb, pb, b_sem, 1, True)

    def value_local(h, _):
        gvs[h] = dot3((wh[h], wl[h]), split(up[h]), TN)
        return 0

    lax.fori_loop(0, H, value_local, 0)
    for l in range(2, L):
        stage(tb, rb, pb, b_sem, l, True)

    def key_grads(h, _):
        later = split(pb[h, 0:FP, :])
        dphi = dot3(split(vs[h]), later, NT)
        dphi = jnp.concatenate([dphi, jnp.zeros((T, FL - FP), F32)], axis=1) + sums_of(pb, h)
        gcon[0:T, LANES : LANES + HK] = gcon[0:T, LANES : LANES + HK] + pull(ks[...], dphi, h)
        gvs[h] = gvs[h] + dot3(split(pk[h][:, :FP]), later, NN)
        return 0

    lax.fori_loop(0, H, key_grads, 0)
    for h in range(H):
        gcon[0:T, (2 + h) * LANES : (3 + h) * LANES] = gvs[h]

    tail = remote(gcon.at[pl.ds(0, RIM)], gcon.at[pl.ds(T, RIM)],
                  (halo_sem.at[1, 0], halo_sem.at[1, 1]), {"seq": prv})
    tail.start()

    def t_hop(l):
        return remote(tt.at[l], tr.at[l], (t_sem.at[l, 0], t_sem.at[l, 1]), {"seq": flip(s, bits[l])})

    grads = gcon[0:T, :]
    tt[0, 0:8, :] = jnp.concatenate(
        [jnp.sum(grads * ext[RIM - j : RIM - j + T, :], axis=0, keepdims=True) for j in range(3)]
        + [jnp.zeros((5, CW), F32)], axis=0)
    t_hop(0).start()

    tail.wait_recv()
    gcon[T : T + RIM, :] = jnp.where(s == n_seq - 1, 0.0, gcon[T : T + RIM, :])

    def conv_back(lo, hi):
        return (taps[0][:, lo:hi] * gcon[0:T, lo:hi] + taps[1][:, lo:hi] * gcon[1 : T + 1, lo:hi]
                + taps[2][:, lo:hi] * gcon[2 : T + 2, lo:hi])

    def t_stage(l):
        t_hop(l).wait_recv()
        tt[l + 1] = tt[l] + tr[l]
        if l + 1 < L:
            t_hop(l + 1).start()

    gq_ref[...] = conv_back(0, LANES)[:, :HK]
    gk_ref[...] = conv_back(LANES, 2 * LANES)[:, :HK]
    t_stage(0)
    gv_ref[...] = conv_back(2 * LANES, CW)
    if L > 1:
        t_stage(1)
    total = m_own[...]
    for r in range(1, n_head):
        m_copy(r).wait_recv()
        total = total + m_recv[r].astype(F32)
    mixed_ref[...] = total.astype(BF16)
    for l in range(2, L):
        t_stage(l)
    gcq_ref[...] = tt[L, 0:3, 0:HK]
    gck_ref[...] = tt[L, 0:3, LANES : LANES + HK]
    gcv_ref[...] = tt[L, 0:3, 2 * LANES :]

    halo.wait_send()
    tail.wait_send()
    for _, copy in og_copies.values():
        copy.wait_send()
    for r in range(1, n_head):
        m_copy(r).wait_send()
    for l in range(L):
        t_hop(l).wait_send()

        def drain(h, _):
            hop(tf, rf, f_sem, l, h).wait_send()
            hop(tb, rb, b_sem, l, h).wait_send()
            return 0

        lax.fori_loop(0, H, drain, 0)


def solution(mesh):
    n_seq, n_head = mesh.shape["seq"], mesh.shape["head"]

    def body(query_in, key_in, value_in, conv_query, conv_key, conv_value, out_proj, out_grad):
        T, HK = query_in.shape
        VC = value_in.shape[1]
        D = out_proj.shape[1]
        H = VC // VD
        fk = HK // H
        pick_a, pick_b, rows, mask, feat = feature_tables(fk, H)
        FL = rows.shape[1]
        FP = round_up(feat, 8)
        FS = FP + 8
        CW = 2 * LANES + VC
        L = n_seq.bit_length() - 1
        TS = T // n_head
        vmem = pl.BlockSpec(memory_space=pltpu.VMEM)
        shape = jax.ShapeDtypeStruct
        big = pltpu.VMEM
        dma = pltpu.SemaphoreType.DMA
        return pl.pallas_call(
            functools.partial(kernel, n_seq, n_head, fk, FP),
            out_shape=(
                shape((TS, D), BF16), shape((T, HK), F32), shape((T, HK), F32), shape((T, VC), F32),
                shape((3, HK), F32), shape((3, HK), F32), shape((3, VC), F32),
            ),
            in_specs=[vmem] * 12,
            out_specs=tuple([vmem] * 7),
            scratch_shapes=[
                big((RIM + T, CW), F32), big((T + RIM, CW), F32),
                big((T, HK), F32), big((T, HK), F32), big((H, T, VD), F32),
                big((H, T, FL), F32), big((H, T, FL), F32),
                big((H, T, T), F32), big((H, T, T), BF16), big((H, T, T), BF16),
                big((H, T, VD), F32), big((H, T, 1), F32), big((H, T, VD), F32),
                big((H, T, 1), F32), big((H, T, VD), BF16), big((H, T, VD), F32),
                big((n_head, TS, D), BF16), big((n_head, TS, D), BF16),
                big((n_head, TS, D), BF16), big((TS, D), F32),
                big((L, H, FS, VD), F32), big((L, H, FS, VD), F32), big((H, FS, VD), F32),
                big((L, H, FS, VD), F32), big((L, H, FS, VD), F32), big((H, FS, VD), F32),
                big((L + 1, 8, CW), F32), big((L, 8, CW), F32),
                dma((2, 2)), dma((n_head, 2)), dma((n_head, 2)),
                dma((L, H, 2)), dma((L, H, 2)), dma((L, 2)),
            ],
            compiler_params=pltpu.CompilerParams(
                collective_id=0, has_side_effects=True, vmem_limit_bytes=58 * 1024 * 1024),
        )(query_in, key_in, value_in, conv_query, conv_key, conv_value, out_proj, out_grad,
          jnp.asarray(pick_a), jnp.asarray(pick_b), jnp.asarray(rows), jnp.asarray(mask))

    in_specs = (
        P("seq", "head"), P("seq", "head"), P("seq", "head"),
        P(None, "head"), P(None, "head"), P(None, "head"),
        P("head", None), P(("seq", "head"), None),
    )
    out_specs = (
        P(("seq", "head"), None), P("seq", "head"), P("seq", "head"), P("seq", "head"),
        P(None, "head"), P(None, "head"), P(None, "head"),
    )
    return jax.shard_map(body, mesh=mesh, in_specs=in_specs, out_specs=out_specs, check_vma=False)
```

```python
import functools
import math

import jax
import jax.numpy as jnp
import ml_dtypes
import numpy as np
from jax import lax
from jax.experimental import pallas as pl
from jax.experimental.pallas import tpu as pltpu
from jax.sharding import PartitionSpec as P

VD = 128
LANES = 128
RIM = 8
MESH = pl.DeviceIdType.MESH
F32, BF16 = jnp.float32, jnp.bfloat16
NN = (((1,), (0,)), ((), ()))
NT = (((1,), (1,)), ((), ()))
TN = (((0,), (0,)), ((), ()))


def round_up(number, step):
    return (number + step - 1) // step * step


def feature_tables(fk, heads):
    feat = fk * (fk + 1) // 2 + fk + 1
    lanes = round_up(feat, LANES)
    pick = np.zeros((heads, 2, heads * fk, 2 * lanes), np.float32)
    rows = np.zeros((8, lanes), np.float32)
    column = 0
    for i in range(fk):
        for j in range(i, fk):
            for h in range(heads):
                pick[h, :, h * fk + i, column] = 1.0
                pick[h, :, h * fk + j, lanes + column] = 1.0
            rows[2, column] = 1.0 / math.sqrt(2.0 * fk if i == j else fk)
            column += 1
    for i in range(fk):
        for h in range(heads):
            pick[h, :, h * fk + i, column] = 1.0
        rows[1, column] = 1.0
        rows[2, column] = fk ** -0.25
        column += 1
    rows[0, column] = rows[1, column] = rows[2, column] = 1.0
    mask = np.zeros((heads, 8, heads * fk), np.float32)
    for h in range(heads):
        mask[h, :, h * fk : (h + 1) * fk] = 1.0
    pick = pick.reshape(heads, 2 * heads * fk, 2 * lanes).astype(ml_dtypes.bfloat16)
    mask3 = np.concatenate([mask] * 3, axis=2).astype(ml_dtypes.bfloat16)
    return pick, rows, mask, np.concatenate([mask3, mask3], axis=1), feat


def dot(a, b, dims):
    return lax.dot_general(a, b, dims, preferred_element_type=F32)


def split(x):
    high = x.astype(BF16)
    return high, (x - high.astype(F32)).astype(BF16)


def beside(*parts):
    return jnp.concatenate(parts, axis=1)


def fold(x):
    half = x.shape[1] // 2
    return x[:, :half] + x[:, half:]


def kernel(n_seq, n_head, fk, feat, FP,
           q_ref, k_ref, v_ref, cq_ref, ck_ref, cv_ref, w_ref, og_ref,
           pick_ref, rows_ref, mask_ref, mask3_ref,
           mixed_ref, gq_ref, gk_ref, gv_ref, gcq_ref, gck_ref, gcv_ref,
           ext, gcon, q3, k3, q2, vcat, aq, bq, ak, bk, dsim, wh, ds_buf,
           num, den, up, gcat, dgr, att, gvs,
           og_all, m_send, m_recv, m_own,
           f_own, f_pair, f_send, f_chain, pf, b_own, b_pair, b_send, b_chain, pb,
           tr, tr_own,
           halo_sem, og_sem, m_sem, f_sem, b_sem, t_send, t_recv):
    HK, T = q_ref.shape
    VC = v_ref.shape[1]
    D = w_ref.shape[1]
    H = VC // VD
    CW = ext.shape[1]
    FL = rows_ref.shape[1]
    TS = T // n_head
    TB = math.gcd(T, 256)
    blocks = range(T // TB)
    Z = n_seq // 2
    s = lax.axis_index("seq")
    h_me = lax.axis_index("head")
    z, odd = s // 2, s % 2

    def flip_all(index, r):
        b = 1
        while b <= r:
            if r & b:
                index = index + b - 2 * b * ((index // b) % 2)
            b *= 2
        return index

    pair = s + 1 - 2 * odd
    nxt = (s + 1) % n_seq
    prv = (s + n_seq - 1) % n_seq

    barrier = pltpu.get_barrier_semaphore()

    def greet(d, _):
        pl.semaphore_signal(barrier, inc=1, device_id={"seq": (s + d) % n_seq}, device_id_type=MESH)
        return 0

    lax.fori_loop(1, n_seq, greet, 0)
    for r in range(1, n_head):
        pl.semaphore_signal(barrier, inc=1, device_id={"head": flip_all(h_me, r)}, device_id_type=MESH)

    zero_rows = jnp.zeros((LANES - HK, T), F32)
    ext[RIM:, 0:LANES] = jnp.concatenate([q_ref[...].astype(F32), zero_rows], axis=0).T
    ext[RIM:, LANES : 2 * LANES] = jnp.concatenate([k_ref[...].astype(F32), zero_rows], axis=0).T
    ext[RIM:, 2 * LANES :] = v_ref[...].astype(F32)

    pl.semaphore_wait(barrier, n_seq - 1 + n_head - 1)

    def remote(src, dst, sem, where):
        return pltpu.make_async_remote_copy(
            src_ref=src, dst_ref=dst, send_sem=sem[0], recv_sem=sem[1],
            device_id=where, device_id_type=MESH)

    halo = remote(ext.at[pl.ds(T, RIM)], ext.at[pl.ds(0, RIM)],
                  (halo_sem.at[0, 0], halo_sem.at[0, 1]), {"seq": nxt})
    halo.start()

    og_copies = {}
    held = [0]
    for b in [1 << i for i in reversed(range(n_head.bit_length() - 1))]:
        for r in held:
            src = og_ref if r == 0 else og_all.at[r]
            og_copies[r ^ b] = (r, remote(src, og_all.at[r ^ b],
                                          (og_sem.at[r ^ b, 0], og_sem.at[r ^ b, 1]),
                                          {"head": flip_all(h_me, b)}))
        held = held + [r ^ b for r in held]
    for r, (src, copy) in og_copies.items():
        if src == 0:
            copy.start()
    og_all[0] = og_ref[...]

    def tap_row(j):
        pad = jnp.zeros((1, LANES - HK), F32)
        return beside(cq_ref[j : j + 1, :], pad, ck_ref[j : j + 1, :], pad, cv_ref[j : j + 1, :])

    taps = [tap_row(j) for j in range(3)]
    row_a, row_b, row_c = (rows_ref[j : j + 1, :] for j in range(3))

    halo.wait_recv()
    ext[0:RIM, :] = jnp.where(s == 0, 0.0, ext[0:RIM, :])

    def conv(lo, hi):
        total = taps[0][:, lo:hi] * ext[RIM : RIM + T, lo:hi]
        total = total + taps[1][:, lo:hi] * ext[RIM - 1 : RIM - 1 + T, lo:hi]
        return total + taps[2][:, lo:hi] * ext[RIM - 2 : RIM - 2 + T, lo:hi]

    high, low = split(conv(LANES, 2 * LANES)[:, :HK])
    k3[...] = beside(high, low, high)
    for h in range(H):
        vcat[h] = beside(*split(conv((2 + h) * LANES, (3 + h) * LANES)))

    def put_state(buf, h, state, total):
        buf[h, :, :] = state
        for c in range(FL // LANES):
            buf[h, feat + c : feat + c + 1, :] = total[:, c * LANES : (c + 1) * LANES]

    def sums_of(buf, h):
        return beside(*[buf[h, feat + c : feat + c + 1, :] for c in range(FL // LANES)])

    def factors(x2, h, a_buf, b_buf):
        both = dot(x2, pick_ref[h], NN)
        a = (both[:, :FL] + row_a) * row_c
        b = both[:, FL:] + row_b
        a_buf[h] = a
        b_buf[h] = b
        return a * b

    def pull(dphi, h, a_buf, b_buf):
        both = beside((dphi * b_buf[h] * row_c).astype(BF16), (dphi * a_buf[h]).astype(BF16))
        return dot(both, pick_ref[h][:HK], NT)

    def to_state(phi, cat):
        high, low = split(phi[:, :FP])
        return fold(dot(high, cat, TN)) + dot(low, cat[:, :VD], TN)

    def by_state(phi, state):
        high, low = split(phi[:, :FP])
        st = beside(*split(state))
        return fold(dot(high, st, NN)) + dot(low, st[:, :VD], NN)

    def on_features(cat, state, total):
        high, low = split(state)
        dphi = dot(cat, beside(high, high), NT) + dot(cat[:, :VD], low, NT)
        return beside(dphi, jnp.zeros((T, FL - FP), F32)) + total

    class Scan:
        def __init__(self, own, pair_buf, send, chain, total, sem, later):
            self.own, self.pair_buf, self.send, self.chain = own, pair_buf, send, chain
            self.total, self.sem, self.later = total, sem, later
            self.place = Z - 1 - z if later else z
            self.wanted = odd == (0 if later else 1)
            self.target = (s + n_seq - 2) % n_seq if later else (s + 2) % n_seq

        def swap(self, h):
            return remote(self.own.at[h], self.pair_buf.at[h],
                          (self.sem.at[0, h, 0], self.sem.at[0, h, 1]), {"seq": pair})

        def pass_on(self, h):
            return remote(self.send.at[h], self.chain.at[h],
                          (self.sem.at[1, h, 0], self.sem.at[1, h, 1]), {"seq": self.target})

        def point(self, p):
            if p >= Z:
                return
            if p == 0:
                def one(h, _):
                    self.swap(h).wait_recv()
                    arrived = self.pair_buf[h]
                    self.total[h] = jnp.where(self.wanted, arrived, 0.0)
                    self.send[h] = self.own[h] + arrived
                    if Z > 1:
                        @pl.when(self.place == 0)
                        def _():
                            self.pass_on(h).start()
                    return 0

                lax.fori_loop(0, H, one, 0)
                return

            @pl.when(self.place == p if p < 3 else self.place >= p)
            def _():
                def one(h, _):
                    self.pass_on(h).wait_recv()
                    arrived = self.chain[h]

                    @pl.when(self.place < Z - 1)
                    def _():
                        self.send[h] = self.send[h] + arrived
                        self.pass_on(h).start()

                    self.total[h] = self.total[h] + arrived
                    return 0

                lax.fori_loop(0, H, one, 0)

        def drain(self):
            def one(h, _):
                self.swap(h).wait_send()

                @pl.when(self.place < Z - 1)
                def _():
                    self.pass_on(h).wait_send()

                return 0

            lax.fori_loop(0, H, one, 0)

    before = Scan(f_own, f_pair, f_send, f_chain, pf, f_sem, False)
    after = Scan(b_own, b_pair, b_send, b_chain, pb, b_sem, True)

    def key_side(h, _):
        phi = factors(k3[:, : 2 * HK], h, ak, bk)
        put_state(f_own, h, to_state(phi, vcat[h]), jnp.sum(phi, axis=0, keepdims=True))
        before.swap(h).start()
        return 0

    lax.fori_loop(0, H, key_side, 0)

    high, low = split(conv(0, LANES)[:, :HK])
    q3[...] = beside(high, high, low)
    q2[...] = beside(high, low)

    def query_side(h, _):
        factors(q2[...], h, aq, bq)
        mine = mask3_ref[h, 0:1, :]
        for i in blocks:
            rows, width = slice(i * TB, (i + 1) * TB), (i + 1) * TB
            sim = dot(q3[rows, :] * mine, k3[0:width, :], NT) * fk ** -0.5
            causal = (lax.broadcasted_iota(jnp.int32, (TB, width), 0) + i * TB
                      >= lax.broadcasted_iota(jnp.int32, (TB, width), 1))
            weights = jnp.where(causal, 1.0 + sim + 0.5 * sim * sim, 0.0).astype(BF16)
            dsim[h, rows, 0:width] = jnp.where(causal, (1.0 + sim) * fk ** -0.5, 0.0)
            wh[h, rows, 0:width] = weights
            den[h, rows, :] = jnp.sum(weights.astype(F32), axis=1, keepdims=True)
            num[h, rows, :] = fold(dot(weights, vcat[h, 0:width, :], NN))
        return 0

    cuts = [0, H // 2, H - H // 4, H]
    lax.fori_loop(cuts[0], cuts[1], query_side, 0)
    before.point(0)
    lax.fori_loop(cuts[1], cuts[2], query_side, 0)
    before.point(1)
    lax.fori_loop(cuts[2], cuts[3], query_side, 0)
    for r, (src, copy) in og_copies.items():
        if src != 0:
            og_copies[src][1].wait_recv()
            copy.start()
    before.point(2)

    forwarded = {src for src, _ in og_copies.values() if src != 0}
    for r in held:
        if r != 0 and r not in forwarded:
            og_copies[r][1].wait_recv()
    for h in range(H):
        product = dot(og_all[...].reshape(T, D), w_ref[h * VD : (h + 1) * VD, :], NT)
        for r in range(n_head):
            first = pl.multiple_of(flip_all(h_me, r) * TS, TS)
            up[h, pl.ds(first, TS), :] = product[r * TS : (r + 1) * TS]
    before.point(3)

    def attend(h, _):
        phi = aq[h] * bq[h]
        denom = den[h] + jnp.sum(phi * sums_of(pf, h), axis=1, keepdims=True)
        inv = 1.0 / denom
        out = (num[h] + by_state(phi, pf[h])) * inv
        att[h] = out.astype(BF16)
        upstream = up[h]
        cat = beside(*split(upstream * inv))
        gcat[h] = cat
        dg = -jnp.sum(upstream * out, axis=1, keepdims=True) * inv
        dgr[h] = dg
        put_state(b_own, h, to_state(phi, cat), jnp.sum(phi * dg, axis=0, keepdims=True))
        after.swap(h).start()
        return 0

    lax.fori_loop(0, H, attend, 0)

    def m_copy(r):
        return remote(m_send.at[r], m_recv.at[r], (m_sem.at[r, 0], m_sem.at[r, 1]),
                      {"head": flip_all(h_me, r)})

    order = sorted(range(n_head), reverse=True)
    mixing = []
    for r in order:
        first = pl.multiple_of(flip_all(h_me, r) * TS, TS)
        mixing.append(beside(*[att[h, pl.ds(first, TS), :] for h in range(H)]))
    mixing = jnp.concatenate(mixing, axis=0)
    step = math.gcd(D, 512)
    for c in range(0, D, step):
        part = dot(mixing, w_ref[:, c : c + step], NN)
        for i, r in enumerate(order):
            piece = part[i * TS : (i + 1) * TS]
            if r:
                m_send[r, :, c : c + step] = piece.astype(BF16)
            else:
                m_own[:, c : c + step] = piece
    for r in order:
        if r:
            m_copy(r).start()

    after.point(0)
    gcon[0:T, 0 : 2 * LANES] = jnp.zeros((T, 2 * LANES), F32)

    def query_grads(h, _):
        cat = gcat[h]
        dg = dgr[h]
        mask = mask_ref[h, 0:1, :]
        gcon[0:T, 0:HK] = gcon[0:T, 0:HK] + pull(
            on_features(cat, pf[h], dg * sums_of(pf, h)), h, aq, bq)
        for i in blocks:
            rows, width = slice(i * TB, (i + 1) * TB), (i + 1) * TB
            vh, vl = vcat[h, 0:width, :VD], vcat[h, 0:width, VD:]
            dw = dot(cat[rows], beside(vh, vh), NT) + dot(cat[rows, :VD], vl, NT) + dg[rows]
            ds = (dw * dsim[h, rows, 0:width]).astype(BF16)
            ds_buf[rows, 0:width] = ds
            gcon[rows, 0:HK] = gcon[rows, 0:HK] + fold(dot(ds, k3[0:width, : 2 * HK], NN)) * mask
        for j in blocks:
            cols = slice(j * TB, (j + 1) * TB)
            gcon[cols, LANES : LANES + HK] = gcon[cols, LANES : LANES + HK] + fold(
                dot(ds_buf[j * TB : T, cols], q2[j * TB : T, :], TN)) * mask
        return 0

    def value_local(h, _):
        for j in blocks:
            cols = slice(j * TB, (j + 1) * TB)
            gvs[h, cols, :] = fold(dot(wh[h, j * TB : T, cols], gcat[h, j * TB : T, :], TN))
        return 0

    lax.fori_loop(0, H // 2, query_grads, 0)
    after.point(1)
    lax.fori_loop(H // 2, H, query_grads, 0)
    after.point(2)
    lax.fori_loop(0, H, value_local, 0)
    after.point(3)

    def key_grads(h, _):
        dphi = on_features(vcat[h], pb[h], sums_of(pb, h))
        gcon[0:T, LANES : LANES + HK] = gcon[0:T, LANES : LANES + HK] + pull(dphi, h, ak, bk)
        gvs[h] = gvs[h] + by_state(ak[h] * bk[h], pb[h])
        return 0

    lax.fori_loop(0, H, key_grads, 0)
    for h in range(H):
        gcon[0:T, (2 + h) * LANES : (3 + h) * LANES] = gvs[h]

    tail = remote(gcon.at[pl.ds(0, RIM)], gcon.at[pl.ds(T, RIM)],
                  (halo_sem.at[1, 0], halo_sem.at[1, 1]), {"seq": prv})
    tail.start()

    grads = gcon[0:T, :]
    tr_own[...] = jnp.concatenate(
        [jnp.sum(grads * ext[RIM - j : RIM - j + T, :], axis=0, keepdims=True) for j in range(3)]
        + [jnp.zeros((5, CW), F32)], axis=0)

    def t_copy(d, at):
        return remote(tr_own, tr.at[at], (t_send.at[d], t_recv.at[at]), {"seq": (s + d) % n_seq})

    def t_start(d, _):
        t_copy(d, s).start()
        return 0

    lax.fori_loop(1, n_seq, t_start, 0)
    tr[s] = tr_own[...]

    total = m_own[...]
    for r in range(1, n_head):
        m_copy(r).wait_recv()
        total = total + m_recv[r].astype(F32)
    mixed_ref[...] = total.astype(BF16)

    tail.wait_recv()
    gcon[T : T + RIM, :] = jnp.where(s == n_seq - 1, 0.0, gcon[T : T + RIM, :])

    def conv_back(lo, hi):
        return (taps[0][:, lo:hi] * gcon[0:T, lo:hi] + taps[1][:, lo:hi] * gcon[1 : T + 1, lo:hi]
                + taps[2][:, lo:hi] * gcon[2 : T + 2, lo:hi])

    gq_ref[...] = conv_back(0, LANES).T[:HK]
    gk_ref[...] = conv_back(LANES, 2 * LANES).T[:HK]
    gv_ref[...] = conv_back(2 * LANES, CW)

    def t_wait(d, _):
        t_copy(d, (s + n_seq - d) % n_seq).wait_recv()
        return 0

    lax.fori_loop(1, n_seq, t_wait, 0)
    tap_grads = lax.fori_loop(1, n_seq, lambda j, acc: acc + tr[j], tr[0])
    gcq_ref[...] = tap_grads[0:3, 0:HK]
    gck_ref[...] = tap_grads[0:3, LANES : LANES + HK]
    gcv_ref[...] = tap_grads[0:3, 2 * LANES :]

    halo.wait_send()
    tail.wait_send()
    for _, copy in og_copies.values():
        copy.wait_send()
    for r in range(1, n_head):
        m_copy(r).wait_send()

    def t_drain(d, _):
        t_copy(d, s).wait_send()
        return 0

    lax.fori_loop(1, n_seq, t_drain, 0)
    before.drain()
    after.drain()


def solution(mesh):
    n_seq, n_head = mesh.shape["seq"], mesh.shape["head"]

    def body(query_in, key_in, value_in, conv_query, conv_key, conv_value, out_proj, out_grad):
        T, HK = query_in.shape
        VC = value_in.shape[1]
        D = out_proj.shape[1]
        H = VC // VD
        fk = HK // H
        pick, rows, mask, mask3, feat = feature_tables(fk, H)
        FL = rows.shape[1]
        FP = round_up(feat + FL // LANES, 16)
        CW = 2 * LANES + VC
        TS = T // n_head
        vmem = pl.BlockSpec(memory_space=pltpu.VMEM)
        shape = jax.ShapeDtypeStruct
        big = pltpu.VMEM
        dma = pltpu.SemaphoreType.DMA
        state = big((H, FP, VD), F32)
        mixed, gq, gk, gv, gcq, gck, gcv = pl.pallas_call(
            functools.partial(kernel, n_seq, n_head, fk, feat, FP),
            out_shape=(
                shape((TS, D), BF16), shape((HK, T), F32), shape((HK, T), F32), shape((T, VC), F32),
                shape((3, HK), F32), shape((3, HK), F32), shape((3, VC), F32),
            ),
            in_specs=[vmem] * 12,
            out_specs=tuple([vmem] * 7),
            scratch_shapes=[
                big((RIM + T, CW), F32), big((T + RIM, CW), F32),
                big((T, 3 * HK), BF16), big((T, 3 * HK), BF16), big((T, 2 * HK), BF16),
                big((H, T, 2 * VD), BF16),
                big((H, T, FL), F32), big((H, T, FL), F32), big((H, T, FL), F32), big((H, T, FL), F32),
                big((H, T, T), F32), big((H, T, T), BF16), big((T, T), BF16),
                big((H, T, VD), F32), big((H, T, 1), F32), big((H, T, VD), F32),
                big((H, T, 2 * VD), BF16), big((H, T, 1), F32), big((H, T, VD), BF16),
                big((H, T, VD), F32),
                big((n_head, TS, D), BF16), big((n_head, TS, D), BF16),
                big((n_head, TS, D), BF16), big((TS, D), F32),
                *[state] * 10,
                big((n_seq, 8, CW), F32), big((8, CW), F32),
                dma((2, 2)), dma((n_head, 2)), dma((n_head, 2)),
                dma((2, H, 2)), dma((2, H, 2)), dma((n_seq,)), dma((n_seq,)),
            ],
            compiler_params=pltpu.CompilerParams(
                collective_id=0, has_side_effects=True, vmem_limit_bytes=58 * 1024 * 1024),
        )(query_in.T, key_in.T, value_in, conv_query, conv_key, conv_value, out_proj, out_grad,
          jnp.asarray(pick), jnp.asarray(rows), jnp.asarray(mask), jnp.asarray(mask3))
        return mixed, gq.T, gk.T, gv, gcq, gck, gcv

    in_specs = (
        P("seq", "head"), P("seq", "head"), P("seq", "head"),
        P(None, "head"), P(None, "head"), P(None, "head"),
        P("head", None), P(("seq", "head"), None),
    )
    out_specs = (
        P(("seq", "head"), None), P("seq", "head"), P("seq", "head"), P("seq", "head"),
        P(None, "head"), P(None, "head"), P(None, "head"),
    )
    return jax.shard_map(body, mesh=mesh, in_specs=in_specs, out_specs=out_specs, check_vma=False)
```

```python
import functools
import math

import jax
import jax.numpy as jnp
import ml_dtypes
import numpy as np
from jax import lax
from jax.experimental import pallas as pl
from jax.experimental.pallas import tpu as pltpu
from jax.sharding import PartitionSpec as P

VD = 128
LANES = 128
RIM = 8
MESH = pl.DeviceIdType.MESH
F32, BF16 = jnp.float32, jnp.bfloat16
NN = (((1,), (0,)), ((), ()))
NT = (((1,), (1,)), ((), ()))
TN = (((0,), (0,)), ((), ()))


def round_up(number, step):
    return (number + step - 1) // step * step


def feature_tables(fk, heads):
    feat = fk * (fk + 1) // 2 + fk + 1
    lanes = round_up(feat, LANES)
    pick = np.zeros((heads, 2, heads * fk, 2 * lanes), np.float32)
    rows = np.zeros((8, lanes), np.float32)
    column = 0
    for i in range(fk):
        for j in range(i, fk):
            for h in range(heads):
                pick[h, :, h * fk + i, column] = 1.0
                pick[h, :, h * fk + j, lanes + column] = 1.0
            rows[2, column] = 1.0 / math.sqrt(2.0 * fk if i == j else fk)
            column += 1
    for i in range(fk):
        for h in range(heads):
            pick[h, :, h * fk + i, column] = 1.0
        rows[1, column] = 1.0
        rows[2, column] = fk ** -0.25
        column += 1
    rows[0, column] = rows[1, column] = rows[2, column] = 1.0
    mask = np.zeros((heads, 8, heads * fk), np.float32)
    for h in range(heads):
        mask[h, :, h * fk : (h + 1) * fk] = 1.0
    pick = pick.reshape(heads, 2 * heads * fk, 2 * lanes).astype(ml_dtypes.bfloat16)
    mask3 = np.concatenate([mask] * 3, axis=2).astype(ml_dtypes.bfloat16)
    return pick, rows, mask, np.concatenate([mask3, mask3], axis=1), feat


def dot(a, b, dims):
    return lax.dot_general(a, b, dims, preferred_element_type=F32)


def split(x):
    high = x.astype(BF16)
    return high, (x - high.astype(F32)).astype(BF16)


def beside(*parts):
    return jnp.concatenate(parts, axis=1)


def fold(x):
    half = x.shape[1] // 2
    return x[:, :half] + x[:, half:]


def tap_rows(cq_ref, ck_ref, cv_ref):
    pad = jnp.zeros((1, LANES - cq_ref.shape[1]), F32)
    return [beside(cq_ref[j : j + 1, :], pad, ck_ref[j : j + 1, :], pad, cv_ref[j : j + 1, :])
            for j in range(3)]


def finish(cq_ref, ck_ref, cv_ref, mixed_in, gcon, tail_ref, taps_ref,
           mixed_ref, gq_ref, gk_ref, gv_ref, gcq_ref, gck_ref, gcv_ref):
    T, CW = gcon.shape
    HK = cq_ref.shape[1]
    taps = tap_rows(cq_ref, ck_ref, cv_ref)

    def conv_back(lo, hi):
        full = jnp.concatenate([gcon[:, lo:hi], tail_ref[:, lo:hi]], axis=0)
        return (taps[0][:, lo:hi] * full[0:T] + taps[1][:, lo:hi] * full[1 : T + 1]
                + taps[2][:, lo:hi] * full[2 : T + 2])

    mixed_ref[...] = mixed_in[...]
    gq_ref[...] = conv_back(0, LANES).T[:HK]
    gk_ref[...] = conv_back(LANES, 2 * LANES).T[:HK]
    for lo in range(2 * LANES, CW, LANES):
        gv_ref[:, lo - 2 * LANES : lo - LANES] = conv_back(lo, lo + LANES)
    gcq_ref[...] = taps_ref[0:3, 0:HK]
    gck_ref[...] = taps_ref[0:3, LANES : LANES + HK]
    gcv_ref[...] = taps_ref[0:3, 2 * LANES :]


def kernel(n_seq, n_head, fk, feat, FP,
           q_ref, k_ref, v_ref, cq_ref, ck_ref, cv_ref, w_ref, og_ref,
           pick_ref, rows_ref, mask_ref, mask3_ref,
           mixed_ref, gcon, tail_ref, taps_ref,
           ext, tail_buf, q3, k3, q2, vcat, aq, bq, ak, bk, dsim, wh, ds_buf,
           num, den, up, gcat, dgr, att, gvs,
           og_all, m_send, m_recv, m_own,
           f_own, f_pair, f_send, f_chain, pf, b_own, b_pair, b_send, b_chain, pb,
           tr, tr_own,
           halo_sem, og_sem, m_sem, f_sem, b_sem, t_send, t_recv):
    HK, T = q_ref.shape
    VC = v_ref.shape[1]
    D = w_ref.shape[1]
    H = VC // VD
    CW = ext.shape[1]
    FL = rows_ref.shape[1]
    TS = T // n_head
    TB = math.gcd(T, 256)
    blocks = range(T // TB)
    Z = n_seq // 2
    s = lax.axis_index("seq")
    h_me = lax.axis_index("head")
    z, odd = s // 2, s % 2

    def flip_all(index, r):
        b = 1
        while b <= r:
            if r & b:
                index = index + b - 2 * b * ((index // b) % 2)
            b *= 2
        return index

    pair = s + 1 - 2 * odd
    nxt = (s + 1) % n_seq
    prv = (s + n_seq - 1) % n_seq

    barrier = pltpu.get_barrier_semaphore()

    def greet(d, _):
        pl.semaphore_signal(barrier, inc=1, device_id={"seq": (s + d) % n_seq}, device_id_type=MESH)
        return 0

    lax.fori_loop(1, n_seq, greet, 0)
    for r in range(1, n_head):
        pl.semaphore_signal(barrier, inc=1, device_id={"head": flip_all(h_me, r)}, device_id_type=MESH)

    zero_rows = jnp.zeros((LANES - HK, T), F32)
    ext[RIM:, 0:LANES] = jnp.concatenate([q_ref[...].astype(F32), zero_rows], axis=0).T
    ext[RIM:, LANES : 2 * LANES] = jnp.concatenate([k_ref[...].astype(F32), zero_rows], axis=0).T
    ext[RIM:, 2 * LANES :] = v_ref[...].astype(F32)

    pl.semaphore_wait(barrier, n_seq - 1 + n_head - 1)

    def remote(src, dst, sem, where):
        return pltpu.make_async_remote_copy(
            src_ref=src, dst_ref=dst, send_sem=sem[0], recv_sem=sem[1],
            device_id=where, device_id_type=MESH)

    halo = remote(ext.at[pl.ds(T, RIM)], ext.at[pl.ds(0, RIM)],
                  (halo_sem.at[0, 0], halo_sem.at[0, 1]), {"seq": nxt})
    halo.start()

    og_copies = {}
    held = [0]
    for b in [1 << i for i in reversed(range(n_head.bit_length() - 1))]:
        for r in held:
            src = og_ref if r == 0 else og_all.at[r]
            og_copies[r ^ b] = (r, remote(src, og_all.at[r ^ b],
                                          (og_sem.at[r ^ b, 0], og_sem.at[r ^ b, 1]),
                                          {"head": flip_all(h_me, b)}))
        held = held + [r ^ b for r in held]
    for r, (src, copy) in og_copies.items():
        if src == 0:
            copy.start()
    og_all[0] = og_ref[...]

    taps = tap_rows(cq_ref, ck_ref, cv_ref)
    row_a, row_b, row_c = (rows_ref[j : j + 1, :] for j in range(3))

    halo.wait_recv()
    ext[0:RIM, :] = jnp.where(s == 0, 0.0, ext[0:RIM, :])

    def conv(lo, hi):
        total = taps[0][:, lo:hi] * ext[RIM : RIM + T, lo:hi]
        total = total + taps[1][:, lo:hi] * ext[RIM - 1 : RIM - 1 + T, lo:hi]
        return total + taps[2][:, lo:hi] * ext[RIM - 2 : RIM - 2 + T, lo:hi]

    high, low = split(conv(LANES, 2 * LANES)[:, :HK])
    k3[...] = beside(high, low, high)
    for h in range(H):
        vcat[h] = beside(*split(conv((2 + h) * LANES, (3 + h) * LANES)))

    def put_state(buf, h, state, total):
        buf[h, :, :] = state
        for c in range(FL // LANES):
            buf[h, feat + c : feat + c + 1, :] = total[:, c * LANES : (c + 1) * LANES]

    def sums_of(buf, h):
        return beside(*[buf[h, feat + c : feat + c + 1, :] for c in range(FL // LANES)])

    def factors(x2, h, a_buf, b_buf):
        both = dot(x2, pick_ref[h], NN)
        a = (both[:, :FL] + row_a) * row_c
        b = both[:, FL:] + row_b
        a_buf[h] = a
        b_buf[h] = b
        return a * b

    def pull(dphi, h, a_buf, b_buf):
        both = beside((dphi * b_buf[h] * row_c).astype(BF16), (dphi * a_buf[h]).astype(BF16))
        return dot(both, pick_ref[h][:HK], NT)

    def to_state(phi, cat):
        high, low = split(phi[:, :FP])
        return fold(dot(high, cat, TN)) + dot(low, cat[:, :VD], TN)

    def by_state(phi, state):
        high, low = split(phi[:, :FP])
        st = beside(*split(state))
        return fold(dot(high, st, NN)) + dot(low, st[:, :VD], NN)

    def on_features(cat, state, total):
        high, low = split(state)
        dphi = dot(cat, beside(high, high), NT) + dot(cat[:, :VD], low, NT)
        return beside(dphi, jnp.zeros((T, FL - FP), F32)) + total

    class Scan:
        def __init__(self, own, pair_buf, send, chain, total, sem, later):
            self.own, self.pair_buf, self.send, self.chain = own, pair_buf, send, chain
            self.total, self.sem, self.later = total, sem, later
            self.place = Z - 1 - z if later else z
            self.wanted = odd == (0 if later else 1)
            self.target = (s + n_seq - 2) % n_seq if later else (s + 2) % n_seq

        def swap(self, h):
            return remote(self.own.at[h], self.pair_buf.at[h],
                          (self.sem.at[0, h, 0], self.sem.at[0, h, 1]), {"seq": pair})

        def pass_on(self, h):
            return remote(self.send.at[h], self.chain.at[h],
                          (self.sem.at[1, h, 0], self.sem.at[1, h, 1]), {"seq": self.target})

        def point(self, p):
            if p >= Z:
                return
            if p == 0:
                def one(h, _):
                    self.swap(h).wait_recv()
                    arrived = self.pair_buf[h]
                    self.total[h] = jnp.where(self.wanted, arrived, 0.0)
                    self.send[h] = self.own[h] + arrived
                    if Z > 1:
                        @pl.when(self.place == 0)
                        def _():
                            self.pass_on(h).start()
                    return 0

                lax.fori_loop(0, H, one, 0)
                return

            @pl.when(self.place == p if p < 3 else self.place >= p)
            def _():
                def one(h, _):
                    self.pass_on(h).wait_recv()
                    arrived = self.chain[h]

                    @pl.when(self.place < Z - 1)
                    def _():
                        self.send[h] = self.send[h] + arrived
                        self.pass_on(h).start()

                    self.total[h] = self.total[h] + arrived
                    return 0

                lax.fori_loop(0, H, one, 0)

        def drain(self):
            def one(h, _):
                self.swap(h).wait_send()

                @pl.when(self.place < Z - 1)
                def _():
                    self.pass_on(h).wait_send()

                return 0

            lax.fori_loop(0, H, one, 0)

    before = Scan(f_own, f_pair, f_send, f_chain, pf, f_sem, False)
    after = Scan(b_own, b_pair, b_send, b_chain, pb, b_sem, True)

    def key_side(h, _):
        phi = factors(k3[:, : 2 * HK], h, ak, bk)
        put_state(f_own, h, to_state(phi, vcat[h]), jnp.sum(phi, axis=0, keepdims=True))
        before.swap(h).start()
        return 0

    lax.fori_loop(0, H, key_side, 0)

    high, low = split(conv(0, LANES)[:, :HK])
    q3[...] = beside(high, high, low)
    q2[...] = beside(high, low)

    def query_side(h, _):
        factors(q2[...], h, aq, bq)
        mine = mask3_ref[h, 0:1, :]
        for i in blocks:
            rows, width = slice(i * TB, (i + 1) * TB), (i + 1) * TB
            sim = dot(q3[rows, :] * mine, k3[0:width, :], NT) * fk ** -0.5
            causal = (lax.broadcasted_iota(jnp.int32, (TB, width), 0) + i * TB
                      >= lax.broadcasted_iota(jnp.int32, (TB, width), 1))
            weights = jnp.where(causal, 1.0 + sim + 0.5 * sim * sim, 0.0).astype(BF16)
            dsim[h, rows, 0:width] = jnp.where(causal, (1.0 + sim) * fk ** -0.5, 0.0)
            wh[h, rows, 0:width] = weights
            den[h, rows, :] = jnp.sum(weights.astype(F32), axis=1, keepdims=True)
            num[h, rows, :] = fold(dot(weights, vcat[h, 0:width, :], NN))
        return 0

    cuts = [0, H // 2, H - H // 4, H]
    lax.fori_loop(cuts[0], cuts[1], query_side, 0)
    before.point(0)
    lax.fori_loop(cuts[1], cuts[2], query_side, 0)
    before.point(1)
    lax.fori_loop(cuts[2], cuts[3], query_side, 0)
    for r, (src, copy) in og_copies.items():
        if src != 0:
            og_copies[src][1].wait_recv()
            copy.start()
    before.point(2)

    forwarded = {src for src, _ in og_copies.values() if src != 0}
    for r in held:
        if r != 0 and r not in forwarded:
            og_copies[r][1].wait_recv()
    for h in range(H):
        product = dot(og_all[...].reshape(T, D), w_ref[h * VD : (h + 1) * VD, :], NT)
        for r in range(n_head):
            first = pl.multiple_of(flip_all(h_me, r) * TS, TS)
            up[h, pl.ds(first, TS), :] = product[r * TS : (r + 1) * TS]
    before.point(3)

    def attend(h, _):
        phi = aq[h] * bq[h]
        denom = den[h] + jnp.sum(phi * sums_of(pf, h), axis=1, keepdims=True)
        inv = 1.0 / denom
        out = (num[h] + by_state(phi, pf[h])) * inv
        att[h] = out.astype(BF16)
        upstream = up[h]
        cat = beside(*split(upstream * inv))
        gcat[h] = cat
        dg = -jnp.sum(upstream * out, axis=1, keepdims=True) * inv
        dgr[h] = dg
        put_state(b_own, h, to_state(phi, cat), jnp.sum(phi * dg, axis=0, keepdims=True))
        after.swap(h).start()
        return 0

    lax.fori_loop(0, H, attend, 0)

    def m_copy(r):
        return remote(m_send.at[r], m_recv.at[r], (m_sem.at[r, 0], m_sem.at[r, 1]),
                      {"head": flip_all(h_me, r)})

    order = sorted(range(n_head), reverse=True)
    mixing = []
    for r in order:
        first = pl.multiple_of(flip_all(h_me, r) * TS, TS)
        mixing.append(beside(*[att[h, pl.ds(first, TS), :] for h in range(H)]))
    mixing = jnp.concatenate(mixing, axis=0)
    step = math.gcd(D, 512)
    for c in range(0, D, step):
        part = dot(mixing, w_ref[:, c : c + step], NN)
        for i, r in enumerate(order):
            piece = part[i * TS : (i + 1) * TS]
            if r:
                m_send[r, :, c : c + step] = piece.astype(BF16)
            else:
                m_own[:, c : c + step] = piece
    for r in order:
        if r:
            m_copy(r).start()

    after.point(0)
    gcon[0:T, 0 : 2 * LANES] = jnp.zeros((T, 2 * LANES), F32)

    def query_grads(h, _):
        cat = gcat[h]
        dg = dgr[h]
        mask = mask_ref[h, 0:1, :]
        gcon[0:T, 0:HK] = gcon[0:T, 0:HK] + pull(
            on_features(cat, pf[h], dg * sums_of(pf, h)), h, aq, bq)
        for i in blocks:
            rows, width = slice(i * TB, (i + 1) * TB), (i + 1) * TB
            vh, vl = vcat[h, 0:width, :VD], vcat[h, 0:width, VD:]
            dw = dot(cat[rows], beside(vh, vh), NT) + dot(cat[rows, :VD], vl, NT) + dg[rows]
            ds = (dw * dsim[h, rows, 0:width]).astype(BF16)
            ds_buf[rows, 0:width] = ds
            gcon[rows, 0:HK] = gcon[rows, 0:HK] + fold(dot(ds, k3[0:width, : 2 * HK], NN)) * mask
        for j in blocks:
            cols = slice(j * TB, (j + 1) * TB)
            gcon[cols, LANES : LANES + HK] = gcon[cols, LANES : LANES + HK] + fold(
                dot(ds_buf[j * TB : T, cols], q2[j * TB : T, :], TN)) * mask
        return 0

    def value_local(h, _):
        for j in blocks:
            cols = slice(j * TB, (j + 1) * TB)
            gvs[h, cols, :] = fold(dot(wh[h, j * TB : T, cols], gcat[h, j * TB : T, :], TN))
        return 0

    lax.fori_loop(0, H // 2, query_grads, 0)
    after.point(1)
    lax.fori_loop(H // 2, H, query_grads, 0)
    after.point(2)
    lax.fori_loop(0, H, value_local, 0)
    after.point(3)

    def key_grads(h, _):
        dphi = on_features(vcat[h], pb[h], sums_of(pb, h))
        gcon[0:T, LANES : LANES + HK] = gcon[0:T, LANES : LANES + HK] + pull(dphi, h, ak, bk)
        gvs[h] = gvs[h] + by_state(ak[h] * bk[h], pb[h])
        return 0

    lax.fori_loop(0, H, key_grads, 0)
    for h in range(H):
        gcon[0:T, (2 + h) * LANES : (3 + h) * LANES] = gvs[h]

    tail = remote(gcon.at[pl.ds(0, RIM)], tail_buf,
                  (halo_sem.at[1, 0], halo_sem.at[1, 1]), {"seq": prv})
    tail.start()

    grads = gcon[0:T, :]
    tr_own[...] = jnp.concatenate(
        [jnp.sum(grads * ext[RIM - j : RIM - j + T, :], axis=0, keepdims=True) for j in range(3)]
        + [jnp.zeros((5, CW), F32)], axis=0)

    def t_copy(d, at):
        return remote(tr_own, tr.at[at], (t_send.at[d], t_recv.at[at]), {"seq": (s + d) % n_seq})

    def t_start(d, _):
        t_copy(d, s).start()
        return 0

    lax.fori_loop(1, n_seq, t_start, 0)
    tr[s] = tr_own[...]

    total = m_own[...]
    for r in range(1, n_head):
        m_copy(r).wait_recv()
        total = total + m_recv[r].astype(F32)
    mixed_ref[...] = total.astype(BF16)

    tail.wait_recv()
    tail_ref[...] = jnp.where(s == n_seq - 1, 0.0, tail_buf[...])

    def t_wait(d, _):
        t_copy(d, (s + n_seq - d) % n_seq).wait_recv()
        return 0

    lax.fori_loop(1, n_seq, t_wait, 0)
    taps_ref[...] = lax.fori_loop(1, n_seq, lambda j, acc: acc + tr[j], tr[0])

    halo.wait_send()
    tail.wait_send()
    for _, copy in og_copies.values():
        copy.wait_send()
    for r in range(1, n_head):
        m_copy(r).wait_send()

    def t_drain(d, _):
        t_copy(d, s).wait_send()
        return 0

    lax.fori_loop(1, n_seq, t_drain, 0)
    before.drain()
    after.drain()


def solution(mesh):
    n_seq, n_head = mesh.shape["seq"], mesh.shape["head"]

    def body(query_in, key_in, value_in, conv_query, conv_key, conv_value, out_proj, out_grad):
        T, HK = query_in.shape
        VC = value_in.shape[1]
        D = out_proj.shape[1]
        H = VC // VD
        fk = HK // H
        pick, rows, mask, mask3, feat = feature_tables(fk, H)
        FL = rows.shape[1]
        FP = round_up(feat + FL // LANES, 16)
        CW = 2 * LANES + VC
        TS = T // n_head
        vmem = pl.BlockSpec(memory_space=pltpu.VMEM)
        shape = jax.ShapeDtypeStruct
        big = pltpu.VMEM
        dma = pltpu.SemaphoreType.DMA
        state = big((H, FP, VD), F32)
        mixed, gcon, tail, tap_sums = pl.pallas_call(
            functools.partial(kernel, n_seq, n_head, fk, feat, FP),
            out_shape=(shape((TS, D), BF16), shape((T, CW), F32), shape((RIM, CW), F32), shape((8, CW), F32)),
            in_specs=[vmem] * 12,
            out_specs=tuple([vmem] * 4),
            scratch_shapes=[
                big((RIM + T, CW), F32), big((RIM, CW), F32),
                big((T, 3 * HK), BF16), big((T, 3 * HK), BF16), big((T, 2 * HK), BF16),
                big((H, T, 2 * VD), BF16),
                big((H, T, FL), F32), big((H, T, FL), F32), big((H, T, FL), F32), big((H, T, FL), F32),
                big((H, T, T), F32), big((H, T, T), BF16), big((T, T), BF16),
                big((H, T, VD), F32), big((H, T, 1), F32), big((H, T, VD), F32),
                big((H, T, 2 * VD), BF16), big((H, T, 1), F32), big((H, T, VD), BF16),
                big((H, T, VD), F32),
                big((n_head, TS, D), BF16), big((n_head, TS, D), BF16),
                big((n_head, TS, D), BF16), big((TS, D), F32),
                *[state] * 10,
                big((n_seq, 8, CW), F32), big((8, CW), F32),
                dma((2, 2)), dma((n_head, 2)), dma((n_head, 2)),
                dma((2, H, 2)), dma((2, H, 2)), dma((n_seq,)), dma((n_seq,)),
            ],
            compiler_params=pltpu.CompilerParams(
                collective_id=0, has_side_effects=True, vmem_limit_bytes=58 * 1024 * 1024),
        )(query_in.T, key_in.T, value_in, conv_query, conv_key, conv_value, out_proj, out_grad,
          jnp.asarray(pick), jnp.asarray(rows), jnp.asarray(mask), jnp.asarray(mask3))
        mixed, gq, gk, gv, gcq, gck, gcv = pl.pallas_call(
            finish,
            out_shape=(
                shape((TS, D), BF16), shape((HK, T), F32), shape((HK, T), F32), shape((T, VC), F32),
                shape((3, HK), F32), shape((3, HK), F32), shape((3, VC), F32),
            ),
            in_specs=[vmem] * 7,
            out_specs=tuple([vmem] * 7),
            compiler_params=pltpu.CompilerParams(vmem_limit_bytes=58 * 1024 * 1024),
        )(conv_query, conv_key, conv_value, mixed, gcon, tail, tap_sums)
        return mixed, gq.T, gk.T, gv, gcq, gck, gcv

    in_specs = (
        P("seq", "head"), P("seq", "head"), P("seq", "head"),
        P(None, "head"), P(None, "head"), P(None, "head"),
        P("head", None), P(("seq", "head"), None),
    )
    out_specs = (
        P(("seq", "head"), None), P("seq", "head"), P("seq", "head"), P("seq", "head"),
        P(None, "head"), P(None, "head"), P(None, "head"),
    )
    return jax.shard_map(body, mesh=mesh, in_specs=in_specs, out_specs=out_specs, check_vma=False)
```

```python
import functools
import math

import jax
import jax.numpy as jnp
import ml_dtypes
import numpy as np
from jax import lax
from jax.experimental import pallas as pl
from jax.experimental.pallas import tpu as pltpu
from jax.sharding import PartitionSpec as P

VD = 128
LANES = 128
RIM = 8
MESH = pl.DeviceIdType.MESH
F32, BF16 = jnp.float32, jnp.bfloat16
NN = (((1,), (0,)), ((), ()))
NT = (((1,), (1,)), ((), ()))
TN = (((0,), (0,)), ((), ()))


def round_up(number, step):
    return (number + step - 1) // step * step


def feature_tables(fk, heads):
    feat = fk * (fk + 1) // 2 + fk + 1
    lanes = round_up(feat, LANES)
    pick = np.zeros((heads, 2, heads * fk, 2 * lanes), np.float32)
    rows = np.zeros((8, lanes), np.float32)
    column = 0
    for i in range(fk):
        for j in range(i, fk):
            for h in range(heads):
                pick[h, :, h * fk + i, column] = 1.0
                pick[h, :, h * fk + j, lanes + column] = 1.0
            rows[2, column] = 1.0 / math.sqrt(2.0 * fk if i == j else fk)
            column += 1
    for i in range(fk):
        for h in range(heads):
            pick[h, :, h * fk + i, column] = 1.0
        rows[1, column] = 1.0
        rows[2, column] = fk ** -0.25
        column += 1
    rows[0, column] = rows[1, column] = rows[2, column] = 1.0
    mask = np.zeros((heads, 8, heads * fk), np.float32)
    for h in range(heads):
        mask[h, :, h * fk : (h + 1) * fk] = 1.0
    pick = pick.reshape(heads, 2 * heads * fk, 2 * lanes).astype(ml_dtypes.bfloat16)
    mask3 = np.concatenate([mask] * 3, axis=2).astype(ml_dtypes.bfloat16)
    return pick, rows, mask, np.concatenate([mask3, mask3], axis=1), feat


def dot(a, b, dims):
    return lax.dot_general(a, b, dims, preferred_element_type=F32)


def split(x):
    high = x.astype(BF16)
    return high, (x - high.astype(F32)).astype(BF16)


def beside(*parts):
    return jnp.concatenate(parts, axis=1)


def fold(x):
    half = x.shape[1] // 2
    return x[:, :half] + x[:, half:]


def tap_rows(cq_ref, ck_ref, cv_ref):
    pad = jnp.zeros((1, LANES - cq_ref.shape[1]), F32)
    return [beside(cq_ref[j : j + 1, :], pad, ck_ref[j : j + 1, :], pad, cv_ref[j : j + 1, :])
            for j in range(3)]


def finish(cq_ref, ck_ref, cv_ref, mixed_in, gcon, tail_ref, taps_ref,
           mixed_ref, gq_ref, gk_ref, gv_ref, gcq_ref, gck_ref, gcv_ref):
    T, CW = gcon.shape
    HK = cq_ref.shape[1]
    taps = tap_rows(cq_ref, ck_ref, cv_ref)

    def conv_back(lo, hi):
        full = jnp.concatenate([gcon[:, lo:hi], tail_ref[:, lo:hi]], axis=0)
        return (taps[0][:, lo:hi] * full[0:T] + taps[1][:, lo:hi] * full[1 : T + 1]
                + taps[2][:, lo:hi] * full[2 : T + 2])

    mixed_ref[...] = mixed_in[...]
    gq_ref[...] = conv_back(0, LANES).T[:HK]
    gk_ref[...] = conv_back(LANES, 2 * LANES).T[:HK]
    for lo in range(2 * LANES, CW, LANES):
        gv_ref[:, lo - 2 * LANES : lo - LANES] = conv_back(lo, lo + LANES)
    gcq_ref[...] = taps_ref[0:3, 0:HK]
    gck_ref[...] = taps_ref[0:3, LANES : LANES + HK]
    gcv_ref[...] = taps_ref[0:3, 2 * LANES :]


def kernel(n_seq, n_head, fk, feat, FP,
           q_ref, k_ref, v_ref, cq_ref, ck_ref, cv_ref, w_hbm, og_ref,
           pick_ref, rows_ref, mask_ref, mask3_ref,
           mixed_ref, gcon, tail_ref, taps_ref,
           ext, tail_buf, q3, k3, q2, vcat, aq, bq, ak, bk, dsim, wh, ds_buf,
           num, den, up, gcat, dgr, att, gvs,
           og_all, m_send, m_recv, m_own,
           f_own, f_pair, f_send, f_chain, f_back, pf, b_own, b_pair, b_send, b_chain, b_back, pb,
           tr, tr_own, taps_buf, w_ref,
           halo_sem, og_sem, m_sem, f_sem, b_sem, t_send, t_recv, w_sem):
    HK, T = q_ref.shape
    VC = v_ref.shape[1]
    D = w_ref.shape[1]
    H = VC // VD
    CW = ext.shape[1]
    FL = rows_ref.shape[1]
    TS = T // n_head
    TB = math.gcd(T, 256)
    blocks = range(T // TB)
    Z = n_seq // 2
    s = lax.axis_index("seq")
    h_me = lax.axis_index("head")
    z, odd = s // 2, s % 2

    def flip_all(index, r):
        b = 1
        while b <= r:
            if r & b:
                index = index + b - 2 * b * ((index // b) % 2)
            b *= 2
        return index

    pair = s + 1 - 2 * odd
    nxt = (s + 1) % n_seq
    prv = (s + n_seq - 1) % n_seq

    barrier = pltpu.get_barrier_semaphore()
    load_w = pltpu.make_async_copy(w_hbm, w_ref, w_sem)
    load_w.start()

    def greet(d, _):
        pl.semaphore_signal(barrier, inc=1, device_id={"seq": (s + d) % n_seq}, device_id_type=MESH)
        return 0

    lax.fori_loop(1, n_seq, greet, 0)
    for r in range(1, n_head):
        pl.semaphore_signal(barrier, inc=1, device_id={"head": flip_all(h_me, r)}, device_id_type=MESH)

    zero_rows = jnp.zeros((LANES - HK, T), F32)
    ext[RIM:, 0:LANES] = jnp.concatenate([q_ref[...].astype(F32), zero_rows], axis=0).T
    ext[RIM:, LANES : 2 * LANES] = jnp.concatenate([k_ref[...].astype(F32), zero_rows], axis=0).T
    ext[RIM:, 2 * LANES :] = v_ref[...].astype(F32)

    pl.semaphore_wait(barrier, n_seq - 1 + n_head - 1)

    def remote(src, dst, sem, where):
        return pltpu.make_async_remote_copy(
            src_ref=src, dst_ref=dst, send_sem=sem[0], recv_sem=sem[1],
            device_id=where, device_id_type=MESH)

    halo = remote(ext.at[pl.ds(T, RIM)], ext.at[pl.ds(0, RIM)],
                  (halo_sem.at[0, 0], halo_sem.at[0, 1]), {"seq": nxt})
    halo.start()

    og_copies = {}
    held = [0]
    for b in [1 << i for i in reversed(range(n_head.bit_length() - 1))]:
        for r in held:
            src = og_ref if r == 0 else og_all.at[r]
            og_copies[r ^ b] = (r, remote(src, og_all.at[r ^ b],
                                          (og_sem.at[r ^ b, 0], og_sem.at[r ^ b, 1]),
                                          {"head": flip_all(h_me, b)}))
        held = held + [r ^ b for r in held]
    for r, (src, copy) in og_copies.items():
        if src == 0:
            copy.start()
    og_all[0] = og_ref[...]

    taps = tap_rows(cq_ref, ck_ref, cv_ref)
    for j in range(3):
        taps_buf[j : j + 1, :] = taps[j]
    row_a, row_b, row_c = (rows_ref[j : j + 1, :] for j in range(3))

    halo.wait_recv()
    ext[0:RIM, :] = jnp.where(s == 0, 0.0, ext[0:RIM, :])

    def conv(lo, hi):
        total = taps[0][:, lo:hi] * ext[RIM : RIM + T, lo:hi]
        total = total + taps[1][:, lo:hi] * ext[RIM - 1 : RIM - 1 + T, lo:hi]
        return total + taps[2][:, lo:hi] * ext[RIM - 2 : RIM - 2 + T, lo:hi]

    high, low = split(conv(LANES, 2 * LANES)[:, :HK])
    k3[...] = beside(high, low, high)

    def put_state(buf, h, state, total):
        buf[h, 0, :, :] = state[: FP // 2]
        buf[h, 1, :, :] = state[FP // 2 :]
        for c in range(FL // LANES):
            half, row = divmod(feat + c, FP // 2)
            buf[h, half, row : row + 1, :] = total[:, c * LANES : (c + 1) * LANES]

    def state_of(buf, h):
        return jnp.concatenate([buf[h, 0], buf[h, 1]], axis=0)

    def sums_of(buf, h):
        rows = [divmod(feat + c, FP // 2) for c in range(FL // LANES)]
        return beside(*[buf[h, half, row : row + 1, :] for half, row in rows])

    def factors(x2, h, a_buf, b_buf):
        both = dot(x2, pick_ref[h], NN)
        a = (both[:, :FL] + row_a) * row_c
        b = both[:, FL:] + row_b
        a_buf[h] = a
        b_buf[h] = b
        return a * b

    def pull(dphi, h, a_buf, b_buf):
        both = beside((dphi * b_buf[h] * row_c).astype(BF16), (dphi * a_buf[h]).astype(BF16))
        return dot(both, pick_ref[h][:HK], NT)

    def to_state(phi, cat):
        high, low = split(phi[:, :FP])
        return fold(dot(high, cat, TN)) + dot(low, cat[:, :VD], TN)

    def by_state(phi, state):
        high, low = split(phi[:, :FP])
        st = beside(*split(state))
        return fold(dot(high, st, NN)) + dot(low, st[:, :VD], NN)

    def on_features(cat, state, total):
        high, low = split(state)
        dphi = dot(cat, beside(high, high), NT) + dot(cat[:, :VD], low, NT)
        return beside(dphi, jnp.zeros((T, FL - FP), F32)) + total

    class Scan:
        def __init__(self, own, pair_buf, send, chain, back, total, sem, later):
            self.own, self.pair_buf, self.send, self.chain = own, pair_buf, send, chain
            self.back, self.total, self.sem = back, total, sem
            self.place = Z - 1 - z if later else z
            self.wanted = odd == (0 if later else 1)
            self.target = (s + n_seq - 2) % n_seq if later else (s + 2) % n_seq

        def link(self, i, h, src, dst, to):
            return remote(src, dst, (self.sem.at[i, h, 0], self.sem.at[i, h, 1]), {"seq": to})

        def swap(self, h):
            return self.link(0, h, self.own.at[h, 1 - odd], self.pair_buf.at[h], pair)

        def pass_on(self, h):
            return self.link(1, h, self.send.at[h], self.chain.at[h], self.target)

        def give_back(self, h):
            return self.link(2, h, self.back.at[h], self.total.at[h, odd], pair)

        def point(self, p):
            if p >= Z:
                return
            if p == 0:
                def one(h, _):
                    self.swap(h).wait_recv()
                    arrived = self.pair_buf[h]
                    mine = self.own[h, odd]
                    self.send[h] = mine + arrived
                    if Z > 1:
                        @pl.when(self.place == 0)
                        def _():
                            self.pass_on(h).start()
                    self.total[h, odd] = jnp.where(self.wanted, arrived, 0.0)
                    self.back[h] = jnp.where(self.wanted, 0.0, mine)

                    @pl.when(self.place == 0)
                    def _():
                        self.give_back(h).start()

                    return 0

                lax.fori_loop(0, H, one, 0)
                return

            @pl.when(self.place == p if p < 3 else self.place >= p)
            def _():
                def one(h, _):
                    self.pass_on(h).wait_recv()
                    arrived = self.chain[h]

                    @pl.when(self.place < Z - 1)
                    def _():
                        self.send[h] = self.send[h] + arrived
                        self.pass_on(h).start()

                    self.back[h] = self.back[h] + arrived
                    self.give_back(h).start()
                    self.total[h, odd] = self.total[h, odd] + arrived
                    return 0

                lax.fori_loop(0, H, one, 0)

        def ready(self, h):
            self.give_back(h).wait_recv()

        def drain(self):
            def one(h, _):
                self.swap(h).wait_send()
                self.give_back(h).wait_send()

                @pl.when(self.place < Z - 1)
                def _():
                    self.pass_on(h).wait_send()

                return 0

            lax.fori_loop(0, H, one, 0)

    before = Scan(f_own, f_pair, f_send, f_chain, f_back, pf, f_sem, False)
    after = Scan(b_own, b_pair, b_send, b_chain, b_back, pb, b_sem, True)

    def key_side(h, _):
        phi = factors(k3[:, : 2 * HK], h, ak, bk)
        lanes = pl.ds(pl.multiple_of((2 + h) * LANES, LANES), LANES)
        value = sum(taps_buf[j : j + 1, lanes] * ext[pl.ds(RIM - j, T), lanes] for j in range(3))
        vcat[h] = beside(*split(value))
        put_state(f_own, h, to_state(phi, vcat[h]), jnp.sum(phi, axis=0, keepdims=True))
        before.swap(h).start()
        return 0

    lax.fori_loop(0, H, key_side, 0)

    high, low = split(conv(0, LANES)[:, :HK])
    q3[...] = beside(high, high, low)
    q2[...] = beside(high, low)

    def query_side(h, _):
        factors(q2[...], h, aq, bq)
        mine = mask3_ref[h, 0:1, :]
        for i in blocks:
            rows, width = slice(i * TB, (i + 1) * TB), (i + 1) * TB
            sim = dot(q3[rows, :] * mine, k3[0:width, :], NT) * fk ** -0.5
            causal = (lax.broadcasted_iota(jnp.int32, (TB, width), 0) + i * TB
                      >= lax.broadcasted_iota(jnp.int32, (TB, width), 1))
            weights = jnp.where(causal, 1.0 + sim + 0.5 * sim * sim, 0.0).astype(BF16)
            dsim[h, rows, 0:width] = jnp.where(causal, (1.0 + sim) * fk ** -0.5, 0.0)
            wh[h, rows, 0:width] = weights
            den[h, rows, :] = jnp.sum(weights.astype(F32), axis=1, keepdims=True)
            num[h, rows, :] = fold(dot(weights, vcat[h, 0:width, :], NN))
        return 0

    cuts = [0, H // 2, H - H // 4, H]
    lax.fori_loop(cuts[0], cuts[1], query_side, 0)
    before.point(0)
    lax.fori_loop(cuts[1], cuts[2], query_side, 0)
    before.point(1)
    lax.fori_loop(cuts[2], cuts[3], query_side, 0)
    for r, (src, copy) in og_copies.items():
        if src != 0:
            og_copies[src][1].wait_recv()
            copy.start()
    before.point(2)

    forwarded = {src for src, _ in og_copies.values() if src != 0}
    for r in held:
        if r != 0 and r not in forwarded:
            og_copies[r][1].wait_recv()
    load_w.wait()
    for h in range(H):
        product = dot(og_all[...].reshape(T, D), w_ref[h * VD : (h + 1) * VD, :], NT)
        for r in range(n_head):
            first = pl.multiple_of(flip_all(h_me, r) * TS, TS)
            up[h, pl.ds(first, TS), :] = product[r * TS : (r + 1) * TS]
    before.point(3)

    def attend(h, _):
        phi = aq[h] * bq[h]
        before.ready(h)
        denom = den[h] + jnp.sum(phi * sums_of(pf, h), axis=1, keepdims=True)
        inv = 1.0 / denom
        out = (num[h] + by_state(phi, state_of(pf, h))) * inv
        att[h] = out.astype(BF16)
        upstream = up[h]
        cat = beside(*split(upstream * inv))
        gcat[h] = cat
        dg = -jnp.sum(upstream * out, axis=1, keepdims=True) * inv
        dgr[h] = dg
        put_state(b_own, h, to_state(phi, cat), jnp.sum(phi * dg, axis=0, keepdims=True))
        after.swap(h).start()
        return 0

    lax.fori_loop(0, H, attend, 0)

    def m_copy(r):
        return remote(m_send.at[r], m_recv.at[r], (m_sem.at[r, 0], m_sem.at[r, 1]),
                      {"head": flip_all(h_me, r)})

    order = sorted(range(n_head), reverse=True)
    mixing = []
    for r in order:
        first = pl.multiple_of(flip_all(h_me, r) * TS, TS)
        mixing.append(beside(*[att[h, pl.ds(first, TS), :] for h in range(H)]))
    mixing = jnp.concatenate(mixing, axis=0)
    step = math.gcd(D, 512)
    for c in range(0, D, step):
        part = dot(mixing, w_ref[:, c : c + step], NN)
        for i, r in enumerate(order):
            piece = part[i * TS : (i + 1) * TS]
            if r:
                m_send[r, :, c : c + step] = piece.astype(BF16)
            else:
                m_own[:, c : c + step] = piece
    for r in order:
        if r:
            m_copy(r).start()

    after.point(0)
    gcon[0:T, 0 : 2 * LANES] = jnp.zeros((T, 2 * LANES), F32)

    def query_grads(h, _):
        cat = gcat[h]
        dg = dgr[h]
        mask = mask_ref[h, 0:1, :]
        gcon[0:T, 0:HK] = gcon[0:T, 0:HK] + pull(
            on_features(cat, state_of(pf, h), dg * sums_of(pf, h)), h, aq, bq)
        for i in blocks:
            rows, width = slice(i * TB, (i + 1) * TB), (i + 1) * TB
            vh, vl = vcat[h, 0:width, :VD], vcat[h, 0:width, VD:]
            dw = dot(cat[rows], beside(vh, vh), NT) + dot(cat[rows, :VD], vl, NT) + dg[rows]
            ds = (dw * dsim[h, rows, 0:width]).astype(BF16)
            ds_buf[rows, 0:width] = ds
            gcon[rows, 0:HK] = gcon[rows, 0:HK] + fold(dot(ds, k3[0:width, : 2 * HK], NN)) * mask
        for j in blocks:
            cols = slice(j * TB, (j + 1) * TB)
            gcon[cols, LANES : LANES + HK] = gcon[cols, LANES : LANES + HK] + fold(
                dot(ds_buf[j * TB : T, cols], q2[j * TB : T, :], TN)) * mask
        return 0

    def value_local(h, _):
        for j in blocks:
            cols = slice(j * TB, (j + 1) * TB)
            gvs[h, cols, :] = fold(dot(wh[h, j * TB : T, cols], gcat[h, j * TB : T, :], TN))
        return 0

    lax.fori_loop(0, H // 2, query_grads, 0)
    after.point(1)
    lax.fori_loop(H // 2, H, query_grads, 0)
    after.point(2)
    lax.fori_loop(0, H, value_local, 0)
    after.point(3)

    def key_grads(h, _):
        after.ready(h)
        dphi = on_features(vcat[h], state_of(pb, h), sums_of(pb, h))
        gcon[0:T, LANES : LANES + HK] = gcon[0:T, LANES : LANES + HK] + pull(dphi, h, ak, bk)
        gvs[h] = gvs[h] + by_state(ak[h] * bk[h], state_of(pb, h))
        return 0

    lax.fori_loop(0, H, key_grads, 0)
    for h in range(H):
        gcon[0:T, (2 + h) * LANES : (3 + h) * LANES] = gvs[h]

    tail = remote(gcon.at[pl.ds(0, RIM)], tail_buf,
                  (halo_sem.at[1, 0], halo_sem.at[1, 1]), {"seq": prv})
    tail.start()

    grads = gcon[0:T, :]
    tr_own[...] = jnp.concatenate(
        [jnp.sum(grads * ext[RIM - j : RIM - j + T, :], axis=0, keepdims=True) for j in range(3)]
        + [jnp.zeros((5, CW), F32)], axis=0)

    def t_copy(d, at):
        return remote(tr_own, tr.at[at], (t_send.at[d], t_recv.at[at]), {"seq": (s + d) % n_seq})

    def t_start(d, _):
        t_copy(d, s).start()
        return 0

    lax.fori_loop(1, n_seq, t_start, 0)
    tr[s] = tr_own[...]

    total = m_own[...]
    for r in range(1, n_head):
        m_copy(r).wait_recv()
        total = total + m_recv[r].astype(F32)
    mixed_ref[...] = total.astype(BF16)

    tail.wait_recv()
    tail_ref[...] = jnp.where(s == n_seq - 1, 0.0, tail_buf[...])

    def t_wait(d, _):
        t_copy(d, (s + n_seq - d) % n_seq).wait_recv()
        return 0

    lax.fori_loop(1, n_seq, t_wait, 0)
    taps_ref[...] = lax.fori_loop(1, n_seq, lambda j, acc: acc + tr[j], tr[0])

    halo.wait_send()
    tail.wait_send()
    for _, copy in og_copies.values():
        copy.wait_send()
    for r in range(1, n_head):
        m_copy(r).wait_send()

    def t_drain(d, _):
        t_copy(d, s).wait_send()
        return 0

    lax.fori_loop(1, n_seq, t_drain, 0)
    before.drain()
    after.drain()


def solution(mesh):
    n_seq, n_head = mesh.shape["seq"], mesh.shape["head"]

    def body(query_in, key_in, value_in, conv_query, conv_key, conv_value, out_proj, out_grad):
        T, HK = query_in.shape
        VC = value_in.shape[1]
        D = out_proj.shape[1]
        H = VC // VD
        fk = HK // H
        pick, rows, mask, mask3, feat = feature_tables(fk, H)
        FL = rows.shape[1]
        FP = round_up(feat + FL // LANES, 16)
        CW = 2 * LANES + VC
        TS = T // n_head
        vmem = pl.BlockSpec(memory_space=pltpu.VMEM)
        shape = jax.ShapeDtypeStruct
        big = pltpu.VMEM
        dma = pltpu.SemaphoreType.DMA
        state, half = big((H, 2, FP // 2, VD), F32), big((H, FP // 2, VD), F32)
        mixed, gcon, tail, tap_sums = pl.pallas_call(
            functools.partial(kernel, n_seq, n_head, fk, feat, FP),
            out_shape=(shape((TS, D), BF16), shape((T, CW), F32), shape((RIM, CW), F32), shape((8, CW), F32)),
            in_specs=[vmem] * 6 + [pl.BlockSpec(memory_space=pl.ANY)] + [vmem] * 5,
            out_specs=tuple([vmem] * 4),
            scratch_shapes=[
                big((RIM + T, CW), F32), big((RIM, CW), F32),
                big((T, 3 * HK), BF16), big((T, 3 * HK), BF16), big((T, 2 * HK), BF16),
                big((H, T, 2 * VD), BF16),
                big((H, T, FL), F32), big((H, T, FL), F32), big((H, T, FL), F32), big((H, T, FL), F32),
                big((H, T, T), F32), big((H, T, T), BF16), big((T, T), BF16),
                big((H, T, VD), F32), big((H, T, 1), F32), big((H, T, VD), F32),
                big((H, T, 2 * VD), BF16), big((H, T, 1), F32), big((H, T, VD), BF16),
                big((H, T, VD), F32),
                big((n_head, TS, D), BF16), big((n_head, TS, D), BF16),
                big((n_head, TS, D), BF16), big((TS, D), F32),
                *[state, half, half, half, half, state] * 2,
                big((n_seq, 8, CW), F32), big((8, CW), F32), big((8, CW), F32), big((VC, D), BF16),
                dma((2, 2)), dma((n_head, 2)), dma((n_head, 2)),
                dma((3, H, 2)), dma((3, H, 2)), dma((n_seq,)), dma((n_seq,)), pltpu.SemaphoreType.DMA(()),
            ],
            compiler_params=pltpu.CompilerParams(
                collective_id=0, has_side_effects=True, vmem_limit_bytes=58 * 1024 * 1024),
        )(query_in.T, key_in.T, value_in, conv_query, conv_key, conv_value, out_proj, out_grad,
          jnp.asarray(pick), jnp.asarray(rows), jnp.asarray(mask), jnp.asarray(mask3))
        mixed, gq, gk, gv, gcq, gck, gcv = pl.pallas_call(
            finish,
            out_shape=(
                shape((TS, D), BF16), shape((HK, T), F32), shape((HK, T), F32), shape((T, VC), F32),
                shape((3, HK), F32), shape((3, HK), F32), shape((3, VC), F32),
            ),
            in_specs=[vmem] * 7,
            out_specs=tuple([vmem] * 7),
            compiler_params=pltpu.CompilerParams(vmem_limit_bytes=58 * 1024 * 1024),
        )(conv_query, conv_key, conv_value, mixed, gcon, tail, tap_sums)
        return mixed, gq.T, gk.T, gv, gcq, gck, gcv

    in_specs = (
        P("seq", "head"), P("seq", "head"), P("seq", "head"),
        P(None, "head"), P(None, "head"), P(None, "head"),
        P("head", None), P(("seq", "head"), None),
    )
    out_specs = (
        P(("seq", "head"), None), P("seq", "head"), P("seq", "head"), P("seq", "head"),
        P(None, "head"), P(None, "head"), P(None, "head"),
    )
    return jax.shard_map(body, mesh=mesh, in_specs=in_specs, out_specs=out_specs, check_vma=False)
```

```python
import functools
import math

import jax
import jax.numpy as jnp
import ml_dtypes
import numpy as np
from jax import lax
from jax.experimental import pallas as pl
from jax.experimental.pallas import tpu as pltpu
from jax.sharding import PartitionSpec as P

VD = 128
LANES = 128
RIM = 8
MESH = pl.DeviceIdType.MESH
F32, BF16 = jnp.float32, jnp.bfloat16
NN = (((1,), (0,)), ((), ()))
NT = (((1,), (1,)), ((), ()))
TN = (((0,), (0,)), ((), ()))


def round_up(number, step):
    return (number + step - 1) // step * step


def feature_tables(fk, heads):
    feat = fk * (fk + 1) // 2 + fk + 1
    lanes = round_up(feat, LANES)
    pick = np.zeros((heads, 2, heads * fk, 2 * lanes), np.float32)
    rows = np.zeros((8, lanes), np.float32)
    column = 0
    for i in range(fk):
        for j in range(i, fk):
            for h in range(heads):
                pick[h, :, h * fk + i, column] = 1.0
                pick[h, :, h * fk + j, lanes + column] = 1.0
            rows[2, column] = 1.0 / math.sqrt(2.0 * fk if i == j else fk)
            column += 1
    for i in range(fk):
        for h in range(heads):
            pick[h, :, h * fk + i, column] = 1.0
        rows[1, column] = 1.0
        rows[2, column] = fk ** -0.25
        column += 1
    rows[0, column] = rows[1, column] = rows[2, column] = 1.0
    mask = np.zeros((heads, 8, heads * fk), np.float32)
    for h in range(heads):
        mask[h, :, h * fk : (h + 1) * fk] = 1.0
    pick = pick.reshape(heads, 2 * heads * fk, 2 * lanes).astype(ml_dtypes.bfloat16)
    mask3 = np.concatenate([mask] * 3, axis=2).astype(ml_dtypes.bfloat16)
    return pick, rows, mask, np.concatenate([mask3, mask3], axis=1), feat


def dot(a, b, dims):
    return lax.dot_general(a, b, dims, preferred_element_type=F32)


def split(x):
    high = x.astype(BF16)
    return high, (x - high.astype(F32)).astype(BF16)


def beside(*parts):
    return jnp.concatenate(parts, axis=1)


def fold(x):
    half = x.shape[1] // 2
    return x[:, :half] + x[:, half:]


def tap_rows(cq_ref, ck_ref, cv_ref):
    pad = jnp.zeros((1, LANES - cq_ref.shape[1]), F32)
    return [beside(cq_ref[j : j + 1, :], pad, ck_ref[j : j + 1, :], pad, cv_ref[j : j + 1, :])
            for j in range(3)]


def finish(cq_ref, ck_ref, cv_ref, mixed_in, gcon, tail_ref, taps_ref,
           mixed_ref, gq_ref, gk_ref, gv_ref, gcq_ref, gck_ref, gcv_ref):
    T, CW = gcon.shape
    HK = cq_ref.shape[1]
    taps = tap_rows(cq_ref, ck_ref, cv_ref)

    def conv_back(lo, hi):
        full = jnp.concatenate([gcon[:, lo:hi], tail_ref[:, lo:hi]], axis=0)
        return (taps[0][:, lo:hi] * full[0:T] + taps[1][:, lo:hi] * full[1 : T + 1]
                + taps[2][:, lo:hi] * full[2 : T + 2])

    mixed_ref[...] = mixed_in[...]
    gq_ref[...] = conv_back(0, LANES).T[:HK]
    gk_ref[...] = conv_back(LANES, 2 * LANES).T[:HK]
    for lo in range(2 * LANES, CW, LANES):
        gv_ref[:, lo - 2 * LANES : lo - LANES] = conv_back(lo, lo + LANES)
    gcq_ref[...] = taps_ref[0:3, 0:HK]
    gck_ref[...] = taps_ref[0:3, LANES : LANES + HK]
    gcv_ref[...] = taps_ref[0:3, 2 * LANES :]


def kernel(n_seq, n_head, fk, feat, FP,
           q_ref, k_ref, v_ref, cq_ref, ck_ref, cv_ref, w_hbm, og_ref,
           pick_ref, rows_ref, mask_ref, mask3_ref,
           mixed_ref, gcon, tail_ref, taps_ref,
           ext, rim, tail_buf, q3, k3, q2, vcat, aq, bq, ak, bk, dsim, draw, wh, ds_buf,
           num, den, up, gcat, dgr, att, gvs,
           og_all, m_send, m_recv, m_own,
           f_own, f_pair, f_send, f_chain, f_back, pf, b_own, b_pair, b_send, b_chain, b_back, pb,
           tr, tr_own, taps_buf, w_ref,
           halo_sem, og_sem, m_sem, f_sem, b_sem, t_send, t_recv, w_sem):
    HK, T = q_ref.shape
    VC = v_ref.shape[1]
    D = w_ref.shape[1]
    H = VC // VD
    CW = ext.shape[1]
    FL = rows_ref.shape[1]
    TS = T // n_head
    TB = math.gcd(T, 256)
    blocks = range(T // TB)
    Z = n_seq // 2
    s = lax.axis_index("seq")
    h_me = lax.axis_index("head")
    z, odd = s // 2, s % 2

    def flip_all(index, r):
        b = 1
        while b <= r:
            if r & b:
                index = index + b - 2 * b * ((index // b) % 2)
            b *= 2
        return index

    pair = s + 1 - 2 * odd
    nxt = (s + 1) % n_seq
    prv = (s + n_seq - 1) % n_seq

    barrier = pltpu.get_barrier_semaphore()
    load_w = pltpu.make_async_copy(w_hbm, w_ref, w_sem)
    load_w.start()

    def greet(d, _):
        pl.semaphore_signal(barrier, inc=1, device_id={"seq": (s + d) % n_seq}, device_id_type=MESH)
        return 0

    lax.fori_loop(1, n_seq, greet, 0)
    for r in range(1, n_head):
        pl.semaphore_signal(barrier, inc=1, device_id={"head": flip_all(h_me, r)}, device_id_type=MESH)

    def upright(block):
        pad = jnp.zeros((LANES - HK, block.shape[1]), F32)
        return jnp.concatenate([block.astype(F32), pad], axis=0).T

    rim[:, 0:LANES] = upright(q_ref[:, T - LANES :])[LANES - RIM :]
    rim[:, LANES : 2 * LANES] = upright(k_ref[:, T - LANES :])[LANES - RIM :]
    rim[:, 2 * LANES :] = v_ref[T - 16 :, :].astype(F32)[16 - RIM :]

    pl.semaphore_wait(barrier, n_seq - 1 + n_head - 1)

    def remote(src, dst, sem, where):
        return pltpu.make_async_remote_copy(
            src_ref=src, dst_ref=dst, send_sem=sem[0], recv_sem=sem[1],
            device_id=where, device_id_type=MESH)

    halo = remote(rim, ext.at[pl.ds(0, RIM)],
                  (halo_sem.at[0, 0], halo_sem.at[0, 1]), {"seq": nxt})
    halo.start()

    og_copies = {}
    held = [0]
    for b in [1 << i for i in reversed(range(n_head.bit_length() - 1))]:
        for r in held:
            src = og_ref if r == 0 else og_all.at[r]
            og_copies[r ^ b] = (r, remote(src, og_all.at[r ^ b],
                                          (og_sem.at[r ^ b, 0], og_sem.at[r ^ b, 1]),
                                          {"head": flip_all(h_me, b)}))
        held = held + [r ^ b for r in held]
    for r, (src, copy) in og_copies.items():
        if src == 0:
            copy.start()
    ext[RIM:, 0:LANES] = upright(q_ref[...])
    ext[RIM:, LANES : 2 * LANES] = upright(k_ref[...])
    ext[RIM:, 2 * LANES :] = v_ref[...].astype(F32)
    og_all[0] = og_ref[...]

    taps = tap_rows(cq_ref, ck_ref, cv_ref)
    for j in range(3):
        taps_buf[j : j + 1, :] = taps[j]
    row_a, row_b, row_c = (rows_ref[j : j + 1, :] for j in range(3))

    halo.wait_recv()
    ext[0:RIM, :] = jnp.where(s == 0, 0.0, ext[0:RIM, :])

    def conv(lo, hi):
        total = taps[0][:, lo:hi] * ext[RIM : RIM + T, lo:hi]
        total = total + taps[1][:, lo:hi] * ext[RIM - 1 : RIM - 1 + T, lo:hi]
        return total + taps[2][:, lo:hi] * ext[RIM - 2 : RIM - 2 + T, lo:hi]

    high, low = split(conv(LANES, 2 * LANES)[:, :HK])
    k3[...] = beside(high, low, high)

    def put_state(buf, h, state, total):
        buf[h, 0, :, :] = state[: FP // 2]
        buf[h, 1, :, :] = state[FP // 2 :]
        for c in range(FL // LANES):
            half, row = divmod(feat + c, FP // 2)
            buf[h, half, row : row + 1, :] = total[:, c * LANES : (c + 1) * LANES]

    def state_of(buf, h):
        return jnp.concatenate([buf[h, 0], buf[h, 1]], axis=0)

    def sums_of(buf, h):
        rows = [divmod(feat + c, FP // 2) for c in range(FL // LANES)]
        return beside(*[buf[h, half, row : row + 1, :] for half, row in rows])

    def factors(x2, h, a_buf, b_buf):
        both = dot(x2, pick_ref[h], NN)
        a = (both[:, :FL] + row_a) * row_c
        b = both[:, FL:] + row_b
        a_buf[h] = a
        b_buf[h] = b
        return a * b

    def pull(dphi, h, a_buf, b_buf):
        both = beside((dphi * b_buf[h] * row_c).astype(BF16), (dphi * a_buf[h]).astype(BF16))
        return dot(both, pick_ref[h][:HK], NT)

    def to_state(phi, cat):
        high, low = split(phi[:, :FP])
        return fold(dot(high, cat, TN)) + dot(low, cat[:, :VD], TN)

    def by_state(phi, state):
        high, low = split(phi[:, :FP])
        st = beside(*split(state))
        return fold(dot(high, st, NN)) + dot(low, st[:, :VD], NN)

    def on_features(cat, state, total):
        high, low = split(state)
        dphi = dot(cat, beside(high, high), NT) + dot(cat[:, :VD], low, NT)
        return beside(dphi, jnp.zeros((T, FL - FP), F32)) + total

    class Scan:
        def __init__(self, own, pair_buf, send, chain, back, total, sem, later):
            self.own, self.pair_buf, self.send, self.chain = own, pair_buf, send, chain
            self.back, self.total, self.sem = back, total, sem
            self.place = Z - 1 - z if later else z
            self.wanted = odd == (0 if later else 1)
            self.target = (s + n_seq - 2) % n_seq if later else (s + 2) % n_seq

        def link(self, i, h, src, dst, to):
            return remote(src, dst, (self.sem.at[i, h, 0], self.sem.at[i, h, 1]), {"seq": to})

        def swap(self, h):
            return self.link(0, h, self.own.at[h, 1 - odd], self.pair_buf.at[h], pair)

        def pass_on(self, h):
            return self.link(1, h, self.send.at[h], self.chain.at[h], self.target)

        def give_back(self, h):
            return self.link(2, h, self.back.at[h], self.total.at[h, odd], pair)

        def point(self, p):
            if p >= Z:
                return
            if p == 0:
                def one(h, _):
                    self.swap(h).wait_recv()
                    arrived = self.pair_buf[h]
                    mine = self.own[h, odd]
                    self.send[h] = mine + arrived
                    if Z > 1:
                        @pl.when(self.place == 0)
                        def _():
                            self.pass_on(h).start()
                    self.total[h, odd] = jnp.where(self.wanted, arrived, 0.0)
                    self.back[h] = jnp.where(self.wanted, 0.0, mine)

                    @pl.when(self.place == 0)
                    def _():
                        self.give_back(h).start()

                    return 0

                lax.fori_loop(0, H, one, 0)
                return

            @pl.when(self.place == p if p < 3 else self.place >= p)
            def _():
                def one(h, _):
                    self.pass_on(h).wait_recv()
                    arrived = self.chain[h]

                    @pl.when(self.place < Z - 1)
                    def _():
                        self.send[h] = self.send[h] + arrived
                        self.pass_on(h).start()

                    self.back[h] = self.back[h] + arrived
                    self.give_back(h).start()
                    self.total[h, odd] = self.total[h, odd] + arrived
                    return 0

                lax.fori_loop(0, H, one, 0)

        def ready(self, h):
            self.give_back(h).wait_recv()

        def drain(self):
            def one(h, _):
                self.swap(h).wait_send()
                self.give_back(h).wait_send()

                @pl.when(self.place < Z - 1)
                def _():
                    self.pass_on(h).wait_send()

                return 0

            lax.fori_loop(0, H, one, 0)

    before = Scan(f_own, f_pair, f_send, f_chain, f_back, pf, f_sem, False)
    after = Scan(b_own, b_pair, b_send, b_chain, b_back, pb, b_sem, True)

    def key_side(h, _):
        phi = factors(k3[:, : 2 * HK], h, ak, bk)
        lanes = pl.ds(pl.multiple_of((2 + h) * LANES, LANES), LANES)
        value = sum(taps_buf[j : j + 1, lanes] * ext[pl.ds(RIM - j, T), lanes] for j in range(3))
        vcat[h] = beside(*split(value))
        put_state(f_own, h, to_state(phi, vcat[h]), jnp.sum(phi, axis=0, keepdims=True))
        before.swap(h).start()
        return 0

    lax.fori_loop(0, H, key_side, 0)

    high, low = split(conv(0, LANES)[:, :HK])
    q3[...] = beside(high, high, low)
    q2[...] = beside(high, low)

    def query_side(h, _):
        factors(q2[...], h, aq, bq)
        mine = mask3_ref[h, 0:1, :]
        for i in blocks:
            rows, width = slice(i * TB, (i + 1) * TB), (i + 1) * TB
            sim = dot(q3[rows, :] * mine, k3[0:width, :], NT) * fk ** -0.5
            causal = (lax.broadcasted_iota(jnp.int32, (TB, width), 0) + i * TB
                      >= lax.broadcasted_iota(jnp.int32, (TB, width), 1))
            weights = jnp.where(causal, 1.0 + sim + 0.5 * sim * sim, 0.0).astype(BF16)
            dsim[h, rows, 0:width] = jnp.where(causal, (1.0 + sim) * fk ** -0.5, 0.0)
            wh[h, rows, 0:width] = weights
            den[h, rows, :] = jnp.sum(weights.astype(F32), axis=1, keepdims=True)
            num[h, rows, :] = fold(dot(weights, vcat[h, 0:width, :], NN))
        return 0

    cuts = [0, H // 2, H - H // 4, H]
    lax.fori_loop(cuts[0], cuts[1], query_side, 0)
    before.point(0)
    lax.fori_loop(cuts[1], cuts[2], query_side, 0)
    before.point(1)
    lax.fori_loop(cuts[2], cuts[3], query_side, 0)
    for r, (src, copy) in og_copies.items():
        if src != 0:
            og_copies[src][1].wait_recv()
            copy.start()
    before.point(2)

    forwarded = {src for src, _ in og_copies.values() if src != 0}
    for r in held:
        if r != 0 and r not in forwarded:
            og_copies[r][1].wait_recv()
    load_w.wait()
    for h in range(H):
        product = dot(og_all[...].reshape(T, D), w_ref[h * VD : (h + 1) * VD, :], NT)
        for r in range(n_head):
            first = pl.multiple_of(flip_all(h_me, r) * TS, TS)
            up[h, pl.ds(first, TS), :] = product[r * TS : (r + 1) * TS]

    def weight_grads(h, _):
        cat = beside(*split(up[h]))
        for i in blocks:
            rows, width = slice(i * TB, (i + 1) * TB), (i + 1) * TB
            vh, vl = vcat[h, 0:width, :VD], vcat[h, 0:width, VD:]
            draw[h, rows, 0:width] = (dot(cat[rows], beside(vh, vh), NT)
                                      + dot(cat[rows, :VD], vl, NT))
        return 0

    lax.fori_loop(0, H, weight_grads, 0)
    before.point(3)

    def attend(h, _):
        phi = aq[h] * bq[h]
        before.ready(h)
        denom = den[h] + jnp.sum(phi * sums_of(pf, h), axis=1, keepdims=True)
        inv = 1.0 / denom
        den[h] = inv
        out = (num[h] + by_state(phi, state_of(pf, h))) * inv
        att[h] = out.astype(BF16)
        upstream = up[h]
        cat = beside(*split(upstream * inv))
        gcat[h] = cat
        dg = -jnp.sum(upstream * out, axis=1, keepdims=True) * inv
        dgr[h] = dg
        put_state(b_own, h, to_state(phi, cat), jnp.sum(phi * dg, axis=0, keepdims=True))
        after.swap(h).start()
        return 0

    lax.fori_loop(0, H, attend, 0)

    def m_copy(r):
        return remote(m_send.at[r], m_recv.at[r], (m_sem.at[r, 0], m_sem.at[r, 1]),
                      {"head": flip_all(h_me, r & -r)})

    def m_take(b):
        for r in range(0, n_head, 2 * b):
            m_copy(r + b).wait_recv()
            m_own[r // 2] = m_own[r // 2] + m_recv[r + b].astype(F32)
        for r in range(2 * b, n_head, 4 * b):
            m_send[r] = m_own[r // 2].astype(BF16)
            m_copy(r).start()

    order = sorted(range(n_head), reverse=True)
    mixing = []
    for r in order:
        first = pl.multiple_of(flip_all(h_me, r) * TS, TS)
        mixing.append(beside(*[att[h, pl.ds(first, TS), :] for h in range(H)]))
    mixing = jnp.concatenate(mixing, axis=0)
    step = math.gcd(D, 512)
    for c in range(0, D, step):
        part = dot(mixing, w_ref[:, c : c + step], NN)
        for i, r in enumerate(order):
            piece = part[i * TS : (i + 1) * TS]
            if r % 2:
                m_send[r, :, c : c + step] = piece.astype(BF16)
            else:
                m_own[r // 2, :, c : c + step] = piece
    for r in order:
        if r % 2:
            m_copy(r).start()

    after.point(0)
    gcon[0:T, 0 : 2 * LANES] = jnp.zeros((T, 2 * LANES), F32)

    def query_grads(h, _):
        cat = gcat[h]
        dg = dgr[h]
        mask = mask_ref[h, 0:1, :]
        gcon[0:T, 0:HK] = gcon[0:T, 0:HK] + pull(
            on_features(cat, state_of(pf, h), dg * sums_of(pf, h)), h, aq, bq)
        for i in blocks:
            rows, width = slice(i * TB, (i + 1) * TB), (i + 1) * TB
            dw = draw[h, rows, 0:width] * den[h, rows, :] + dg[rows]
            ds = (dw * dsim[h, rows, 0:width]).astype(BF16)
            ds_buf[rows, 0:width] = ds
            gcon[rows, 0:HK] = gcon[rows, 0:HK] + fold(dot(ds, k3[0:width, : 2 * HK], NN)) * mask
        for j in blocks:
            cols = slice(j * TB, (j + 1) * TB)
            gcon[cols, LANES : LANES + HK] = gcon[cols, LANES : LANES + HK] + fold(
                dot(ds_buf[j * TB : T, cols], q2[j * TB : T, :], TN)) * mask
        return 0

    def value_local(h, _):
        for j in blocks:
            cols = slice(j * TB, (j + 1) * TB)
            gvs[h, cols, :] = fold(dot(wh[h, j * TB : T, cols], gcat[h, j * TB : T, :], TN))
        return 0

    head_bits = [1 << i for i in range(n_head.bit_length() - 1)]
    lax.fori_loop(0, H // 4, query_grads, 0)
    m_take(head_bits[0])
    lax.fori_loop(H // 4, H // 2, query_grads, 0)
    after.point(1)
    lax.fori_loop(H // 2, H, query_grads, 0)
    after.point(2)
    lax.fori_loop(0, H, value_local, 0)
    after.point(3)

    def key_grads(h, _):
        after.ready(h)
        dphi = on_features(vcat[h], state_of(pb, h), sums_of(pb, h))
        gcon[0:T, LANES : LANES + HK] = gcon[0:T, LANES : LANES + HK] + pull(dphi, h, ak, bk)
        gvs[h] = gvs[h] + by_state(ak[h] * bk[h], state_of(pb, h))
        return 0

    lax.fori_loop(0, H, key_grads, 0)
    for h in range(H):
        gcon[0:T, (2 + h) * LANES : (3 + h) * LANES] = gvs[h]

    tail = remote(gcon.at[pl.ds(0, RIM)], tail_buf,
                  (halo_sem.at[1, 0], halo_sem.at[1, 1]), {"seq": prv})
    tail.start()

    grads = gcon[0:T, :]
    tr_own[...] = jnp.concatenate(
        [jnp.sum(grads * ext[RIM - j : RIM - j + T, :], axis=0, keepdims=True) for j in range(3)]
        + [jnp.zeros((5, CW), F32)], axis=0)

    def t_copy(d, at):
        return remote(tr_own, tr.at[at], (t_send.at[d], t_recv.at[at]), {"seq": (s + d) % n_seq})

    def t_start(d, _):
        t_copy(d, s).start()
        return 0

    lax.fori_loop(1, n_seq, t_start, 0)
    tr[s] = tr_own[...]

    for b in head_bits[1:]:
        m_take(b)
    mixed_ref[...] = m_own[0].astype(BF16)

    tail.wait_recv()
    tail_ref[...] = jnp.where(s == n_seq - 1, 0.0, tail_buf[...])

    def t_wait(d, _):
        t_copy(d, (s + n_seq - d) % n_seq).wait_recv()
        return 0

    lax.fori_loop(1, n_seq, t_wait, 0)
    taps_ref[...] = lax.fori_loop(1, n_seq, lambda j, acc: acc + tr[j], tr[0])

    halo.wait_send()
    tail.wait_send()
    for _, copy in og_copies.values():
        copy.wait_send()
    for r in range(1, n_head):
        m_copy(r).wait_send()

    def t_drain(d, _):
        t_copy(d, s).wait_send()
        return 0

    lax.fori_loop(1, n_seq, t_drain, 0)
    before.drain()
    after.drain()


def solution(mesh):
    n_seq, n_head = mesh.shape["seq"], mesh.shape["head"]

    def body(query_in, key_in, value_in, conv_query, conv_key, conv_value, out_proj, out_grad):
        T, HK = query_in.shape
        VC = value_in.shape[1]
        D = out_proj.shape[1]
        H = VC // VD
        fk = HK // H
        pick, rows, mask, mask3, feat = feature_tables(fk, H)
        FL = rows.shape[1]
        FP = round_up(feat + FL // LANES, 16)
        CW = 2 * LANES + VC
        TS = T // n_head
        vmem = pl.BlockSpec(memory_space=pltpu.VMEM)
        shape = jax.ShapeDtypeStruct
        big = pltpu.VMEM
        dma = pltpu.SemaphoreType.DMA
        state, half = big((H, 2, FP // 2, VD), F32), big((H, FP // 2, VD), F32)
        mixed, gcon, tail, tap_sums = pl.pallas_call(
            functools.partial(kernel, n_seq, n_head, fk, feat, FP),
            out_shape=(shape((TS, D), BF16), shape((T, CW), F32), shape((RIM, CW), F32), shape((8, CW), F32)),
            in_specs=[vmem] * 6 + [pl.BlockSpec(memory_space=pl.ANY)] + [vmem] * 5,
            out_specs=tuple([vmem] * 4),
            scratch_shapes=[
                big((RIM + T, CW), F32), big((RIM, CW), F32), big((RIM, CW), F32),
                big((T, 3 * HK), BF16), big((T, 3 * HK), BF16), big((T, 2 * HK), BF16),
                big((H, T, 2 * VD), BF16),
                big((H, T, FL), F32), big((H, T, FL), F32), big((H, T, FL), F32), big((H, T, FL), F32),
                big((H, T, T), F32), big((H, T, T), F32), big((H, T, T), BF16), big((T, T), BF16),
                big((H, T, VD), F32), big((H, T, 1), F32), big((H, T, VD), F32),
                big((H, T, 2 * VD), BF16), big((H, T, 1), F32), big((H, T, VD), BF16),
                big((H, T, VD), F32),
                big((n_head, TS, D), BF16), big((n_head, TS, D), BF16),
                big((n_head, TS, D), BF16), big((n_head // 2, TS, D), F32),
                *[state, half, half, half, half, state] * 2,
                big((n_seq, 8, CW), F32), big((8, CW), F32), big((8, CW), F32), big((VC, D), BF16),
                dma((2, 2)), dma((n_head, 2)), dma((n_head, 2)),
                dma((3, H, 2)), dma((3, H, 2)), dma((n_seq,)), dma((n_seq,)), pltpu.SemaphoreType.DMA(()),
            ],
            compiler_params=pltpu.CompilerParams(
                collective_id=0, has_side_effects=True, vmem_limit_bytes=58 * 1024 * 1024),
        )(query_in.T, key_in.T, value_in, conv_query, conv_key, conv_value, out_proj, out_grad,
          jnp.asarray(pick), jnp.asarray(rows), jnp.asarray(mask), jnp.asarray(mask3))
        mixed, gq, gk, gv, gcq, gck, gcv = pl.pallas_call(
            finish,
            out_shape=(
                shape((TS, D), BF16), shape((HK, T), F32), shape((HK, T), F32), shape((T, VC), F32),
                shape((3, HK), F32), shape((3, HK), F32), shape((3, VC), F32),
            ),
            in_specs=[vmem] * 7,
            out_specs=tuple([vmem] * 7),
            compiler_params=pltpu.CompilerParams(vmem_limit_bytes=58 * 1024 * 1024),
        )(conv_query, conv_key, conv_value, mixed, gcon, tail, tap_sums)
        return mixed, gq.T, gk.T, gv, gcq, gck, gcv

    in_specs = (
        P("seq", "head"), P("seq", "head"), P("seq", "head"),
        P(None, "head"), P(None, "head"), P(None, "head"),
        P("head", None), P(("seq", "head"), None),
    )
    out_specs = (
        P(("seq", "head"), None), P("seq", "head"), P("seq", "head"), P("seq", "head"),
        P(None, "head"), P(None, "head"), P(None, "head"),
    )
    return jax.shard_map(body, mesh=mesh, in_specs=in_specs, out_specs=out_specs, check_vma=False)
```

```python
import functools
import math

import jax
import jax.numpy as jnp
import ml_dtypes
import numpy as np
from jax import lax
from jax.experimental import pallas as pl
from jax.experimental.pallas import tpu as pltpu
from jax.sharding import PartitionSpec as P

VD = 128
LANES = 128
RIM = 8
MESH = pl.DeviceIdType.MESH
F32, BF16 = jnp.float32, jnp.bfloat16
NN = (((1,), (0,)), ((), ()))
NT = (((1,), (1,)), ((), ()))
TN = (((0,), (0,)), ((), ()))


def round_up(number, step):
    return (number + step - 1) // step * step


def feature_tables(fk, heads):
    feat = fk * (fk + 1) // 2 + fk + 1
    lanes = round_up(feat, LANES)
    pick = np.zeros((heads, 2, heads * fk, 2 * lanes), np.float32)
    rows = np.zeros((8, lanes), np.float32)
    column = 0
    for i in range(fk):
        for j in range(i, fk):
            for h in range(heads):
                pick[h, :, h * fk + i, column] = 1.0
                pick[h, :, h * fk + j, lanes + column] = 1.0
            rows[2, column] = 1.0 / math.sqrt(2.0 * fk if i == j else fk)
            column += 1
    for i in range(fk):
        for h in range(heads):
            pick[h, :, h * fk + i, column] = 1.0
        rows[1, column] = 1.0
        rows[2, column] = fk ** -0.25
        column += 1
    rows[0, column] = rows[1, column] = rows[2, column] = 1.0
    mask = np.zeros((heads, 8, heads * fk), np.float32)
    for h in range(heads):
        mask[h, :, h * fk : (h + 1) * fk] = 1.0
    pick = pick.reshape(heads, 2 * heads * fk, 2 * lanes).astype(ml_dtypes.bfloat16)
    mask3 = np.concatenate([mask] * 3, axis=2).astype(ml_dtypes.bfloat16)
    return pick, rows, mask, np.concatenate([mask3, mask3], axis=1), feat


def dot(a, b, dims):
    return lax.dot_general(a, b, dims, preferred_element_type=F32)


def split(x):
    high = x.astype(BF16)
    return high, (x - high.astype(F32)).astype(BF16)


def beside(*parts):
    return jnp.concatenate(parts, axis=1)


def fold(x):
    half = x.shape[1] // 2
    return x[:, :half] + x[:, half:]


def tap_rows(cq_ref, ck_ref, cv_ref):
    pad = jnp.zeros((1, LANES - cq_ref.shape[1]), F32)
    return [beside(cq_ref[j : j + 1, :], pad, ck_ref[j : j + 1, :], pad, cv_ref[j : j + 1, :])
            for j in range(3)]


def finish(cq_ref, ck_ref, cv_ref, mixed_in, gcon, tail_ref, taps_ref,
           mixed_ref, gq_ref, gk_ref, gv_ref, gcq_ref, gck_ref, gcv_ref):
    T, CW = gcon.shape
    HK = cq_ref.shape[1]
    taps = tap_rows(cq_ref, ck_ref, cv_ref)

    def conv_back(lo, hi):
        full = jnp.concatenate([gcon[:, lo:hi], tail_ref[:, lo:hi]], axis=0)
        return (taps[0][:, lo:hi] * full[0:T] + taps[1][:, lo:hi] * full[1 : T + 1]
                + taps[2][:, lo:hi] * full[2 : T + 2])

    mixed_ref[...] = mixed_in[...]
    gq_ref[...] = conv_back(0, LANES).T[:HK]
    gk_ref[...] = conv_back(LANES, 2 * LANES).T[:HK]
    for lo in range(2 * LANES, CW, LANES):
        gv_ref[:, lo - 2 * LANES : lo - LANES] = conv_back(lo, lo + LANES)
    gcq_ref[...] = taps_ref[0:3, 0:HK]
    gck_ref[...] = taps_ref[0:3, LANES : LANES + HK]
    gcv_ref[...] = taps_ref[0:3, 2 * LANES :]


def kernel(n_seq, n_head, fk, feat, FP,
           q_ref, k_ref, v_ref, cq_ref, ck_ref, cv_ref, w_hbm, og_ref,
           pick_ref, rows_ref, mask_ref, mask3_ref,
           mixed_ref, gcon, tail_ref, taps_ref,
           ext, rim, tail_buf, q3, k3, q2, vcat, aq, bq, ak, bk, dsim, draw, wh, ds_buf,
           num, den, up, gcat, dgr, att, gvs,
           og_all, m_send, m_recv, m_own,
           f_own, f_pair, f_send, f_chain, f_back, pf, b_own, b_pair, b_send, b_chain, b_back, pb,
           tr, tr_own, taps_buf, w_ref,
           halo_sem, og_sem, m_sem, f_sem, b_sem, t_send, t_recv, w_sem):
    HK, T = q_ref.shape
    VC = v_ref.shape[1]
    D = w_ref.shape[1]
    H = VC // VD
    CW = ext.shape[1]
    FL = rows_ref.shape[1]
    TS = T // n_head
    TB = math.gcd(T, 256)
    blocks = range(T // TB)
    Z = n_seq // 2
    s = lax.axis_index("seq")
    h_me = lax.axis_index("head")
    z, odd = s // 2, s % 2

    def flip_all(index, r):
        b = 1
        while b <= r:
            if r & b:
                index = index + b - 2 * b * ((index // b) % 2)
            b *= 2
        return index

    pair = s + 1 - 2 * odd
    nxt = (s + 1) % n_seq
    prv = (s + n_seq - 1) % n_seq

    barrier = pltpu.get_barrier_semaphore()
    load_w = pltpu.make_async_copy(w_hbm, w_ref, w_sem)
    load_w.start()

    def greet(d, _):
        pl.semaphore_signal(barrier, inc=1, device_id={"seq": (s + d) % n_seq}, device_id_type=MESH)
        return 0

    lax.fori_loop(1, n_seq, greet, 0)
    for r in range(1, n_head):
        pl.semaphore_signal(barrier, inc=1, device_id={"head": flip_all(h_me, r)}, device_id_type=MESH)

    def upright(block):
        pad = jnp.zeros((LANES - HK, block.shape[1]), F32)
        return jnp.concatenate([block.astype(F32), pad], axis=0).T

    rim[:, 0:LANES] = upright(q_ref[:, T - LANES :])[LANES - RIM :]
    rim[:, LANES : 2 * LANES] = upright(k_ref[:, T - LANES :])[LANES - RIM :]
    rim[:, 2 * LANES :] = v_ref[T - 16 :, :].astype(F32)[16 - RIM :]

    pl.semaphore_wait(barrier, n_seq - 1 + n_head - 1)

    def remote(src, dst, sem, where):
        return pltpu.make_async_remote_copy(
            src_ref=src, dst_ref=dst, send_sem=sem[0], recv_sem=sem[1],
            device_id=where, device_id_type=MESH)

    halo = remote(rim, ext.at[pl.ds(0, RIM)],
                  (halo_sem.at[0, 0], halo_sem.at[0, 1]), {"seq": nxt})
    halo.start()

    og_copies = {}
    held = [0]
    for b in [1 << i for i in reversed(range(n_head.bit_length() - 1))]:
        for r in held:
            src = og_ref if r == 0 else og_all.at[r]
            og_copies[r ^ b] = (r, remote(src, og_all.at[r ^ b],
                                          (og_sem.at[r ^ b, 0], og_sem.at[r ^ b, 1]),
                                          {"head": flip_all(h_me, b)}))
        held = held + [r ^ b for r in held]
    for r, (src, copy) in og_copies.items():
        if src == 0:
            copy.start()
    ext[RIM:, 0:LANES] = upright(q_ref[...])
    ext[RIM:, LANES : 2 * LANES] = upright(k_ref[...])
    ext[RIM:, 2 * LANES :] = v_ref[...].astype(F32)
    og_all[0] = og_ref[...]

    taps = tap_rows(cq_ref, ck_ref, cv_ref)
    for j in range(3):
        taps_buf[j : j + 1, :] = taps[j]
    row_a, row_b, row_c = (rows_ref[j : j + 1, :] for j in range(3))

    halo.wait_recv()
    ext[0:RIM, :] = jnp.where(s == 0, 0.0, ext[0:RIM, :])

    def conv(lo, hi):
        total = taps[0][:, lo:hi] * ext[RIM : RIM + T, lo:hi]
        total = total + taps[1][:, lo:hi] * ext[RIM - 1 : RIM - 1 + T, lo:hi]
        return total + taps[2][:, lo:hi] * ext[RIM - 2 : RIM - 2 + T, lo:hi]

    high, low = split(conv(LANES, 2 * LANES)[:, :HK])
    k3[...] = beside(high, low, high)

    def put_state(buf, h, state, total):
        buf[h, 0, :, :] = state[: FP // 2]
        buf[h, 1, :, :] = state[FP // 2 :]
        for c in range(FL // LANES):
            half, row = divmod(feat + c, FP // 2)
            buf[h, half, row : row + 1, :] = total[:, c * LANES : (c + 1) * LANES]

    def state_of(buf, h):
        return jnp.concatenate([buf[h, 0], buf[h, 1]], axis=0)

    def sums_of(buf, h):
        rows = [divmod(feat + c, FP // 2) for c in range(FL // LANES)]
        return beside(*[buf[h, half, row : row + 1, :] for half, row in rows])

    def factors(x2, h, a_buf, b_buf):
        both = dot(x2, pick_ref[h], NN)
        a = (both[:, :FL] + row_a) * row_c
        b = both[:, FL:] + row_b
        a_buf[h] = a
        b_buf[h] = b
        return a * b

    def pull(dphi, h, a_buf, b_buf):
        both = beside((dphi * b_buf[h] * row_c).astype(BF16), (dphi * a_buf[h]).astype(BF16))
        return dot(both, pick_ref[h][:HK], NT)

    def to_state(phi, cat):
        high, low = split(phi[:, :FP])
        return fold(dot(high, cat, TN)) + dot(low, cat[:, :VD], TN)

    def by_state(phi, state):
        high, low = split(phi[:, :FP])
        st = beside(*split(state))
        return fold(dot(high, st, NN)) + dot(low, st[:, :VD], NN)

    def on_features(cat, state, total):
        high, low = split(state)
        dphi = dot(cat, beside(high, high), NT) + dot(cat[:, :VD], low, NT)
        return beside(dphi, jnp.zeros((T, FL - FP), F32)) + total

    class Scan:
        def __init__(self, own, pair_buf, send, chain, back, total, sem, later):
            self.own, self.pair_buf, self.send, self.chain = own, pair_buf, send, chain
            self.back, self.total, self.sem = back, total, sem
            self.place = Z - 1 - z if later else z
            self.wanted = odd == (0 if later else 1)
            self.target = (s + n_seq - 2) % n_seq if later else (s + 2) % n_seq

        def link(self, i, h, src, dst, to):
            return remote(src, dst, (self.sem.at[i, h, 0], self.sem.at[i, h, 1]), {"seq": to})

        def swap(self, h):
            return self.link(0, h, self.own.at[h, 1 - odd], self.pair_buf.at[h], pair)

        def pass_on(self, h):
            return self.link(1, h, self.send.at[h], self.chain.at[h], self.target)

        def give_back(self, h):
            return self.link(2, h, self.back.at[h], self.total.at[h, odd], pair)

        def point(self, p):
            if p >= Z:
                return
            if p == 0:
                def one(h, _):
                    self.swap(h).wait_recv()
                    arrived = self.pair_buf[h]
                    mine = self.own[h, odd]
                    self.send[h] = mine + arrived
                    if Z > 1:
                        @pl.when(self.place == 0)
                        def _():
                            self.pass_on(h).start()
                    self.total[h, odd] = jnp.where(self.wanted, arrived, 0.0)
                    self.back[h] = jnp.where(self.wanted, 0.0, mine)

                    @pl.when(self.place == 0)
                    def _():
                        self.give_back(h).start()

                    return 0

                lax.fori_loop(0, H, one, 0)
                return

            @pl.when(self.place == p if p < 3 else self.place >= p)
            def _():
                def one(h, _):
                    self.pass_on(h).wait_recv()
                    arrived = self.chain[h]

                    @pl.when(self.place < Z - 1)
                    def _():
                        self.send[h] = self.send[h] + arrived
                        self.pass_on(h).start()

                    self.back[h] = self.back[h] + arrived
                    self.give_back(h).start()
                    self.total[h, odd] = self.total[h, odd] + arrived
                    return 0

                lax.fori_loop(0, H, one, 0)

        def ready(self, h):
            self.give_back(h).wait_recv()

        def drain(self):
            def one(h, _):
                self.swap(h).wait_send()
                self.give_back(h).wait_send()

                @pl.when(self.place < Z - 1)
                def _():
                    self.pass_on(h).wait_send()

                return 0

            lax.fori_loop(0, H, one, 0)

    before = Scan(f_own, f_pair, f_send, f_chain, f_back, pf, f_sem, False)
    after = Scan(b_own, b_pair, b_send, b_chain, b_back, pb, b_sem, True)

    def key_side(h, _):
        phi = factors(k3[:, : 2 * HK], h, ak, bk)
        lanes = pl.ds(pl.multiple_of((2 + h) * LANES, LANES), LANES)
        value = sum(taps_buf[j : j + 1, lanes] * ext[pl.ds(RIM - j, T), lanes] for j in range(3))
        vcat[h] = beside(*split(value))
        put_state(f_own, h, to_state(phi, vcat[h]), jnp.sum(phi, axis=0, keepdims=True))
        before.swap(h).start()
        return 0

    lax.fori_loop(0, H, key_side, 0, unroll=True)

    high, low = split(conv(0, LANES)[:, :HK])
    q3[...] = beside(high, high, low)
    q2[...] = beside(high, low)

    def query_side(h, _):
        factors(q2[...], h, aq, bq)
        mine = mask3_ref[h, 0:1, :]
        for i in blocks:
            rows, width = slice(i * TB, (i + 1) * TB), (i + 1) * TB
            sim = dot(q3[rows, :] * mine, k3[0:width, :], NT) * fk ** -0.5
            causal = (lax.broadcasted_iota(jnp.int32, (TB, width), 0) + i * TB
                      >= lax.broadcasted_iota(jnp.int32, (TB, width), 1))
            weights = jnp.where(causal, 1.0 + sim + 0.5 * sim * sim, 0.0).astype(BF16)
            dsim[h, rows, 0:width] = jnp.where(causal, (1.0 + sim) * fk ** -0.5, 0.0)
            wh[h, rows, 0:width] = weights
            den[h, rows, :] = jnp.sum(weights.astype(F32), axis=1, keepdims=True)
            num[h, rows, :] = fold(dot(weights, vcat[h, 0:width, :], NN))
        return 0

    cuts = [0, H // 2, H - H // 4, H]
    lax.fori_loop(cuts[0], cuts[1], query_side, 0, unroll=True)
    before.point(0)
    lax.fori_loop(cuts[1], cuts[2], query_side, 0, unroll=True)
    before.point(1)
    lax.fori_loop(cuts[2], cuts[3], query_side, 0, unroll=True)
    for r, (src, copy) in og_copies.items():
        if src != 0:
            og_copies[src][1].wait_recv()
            copy.start()
    before.point(2)

    forwarded = {src for src, _ in og_copies.values() if src != 0}
    for r in held:
        if r != 0 and r not in forwarded:
            og_copies[r][1].wait_recv()
    load_w.wait()
    for h in range(H):
        product = dot(og_all[...].reshape(T, D), w_ref[h * VD : (h + 1) * VD, :], NT)
        for r in range(n_head):
            first = pl.multiple_of(flip_all(h_me, r) * TS, TS)
            up[h, pl.ds(first, TS), :] = product[r * TS : (r + 1) * TS]

    def weight_grads(h, _):
        cat = beside(*split(up[h]))
        for i in blocks:
            rows, width = slice(i * TB, (i + 1) * TB), (i + 1) * TB
            vh, vl = vcat[h, 0:width, :VD], vcat[h, 0:width, VD:]
            draw[h, rows, 0:width] = (dot(cat[rows], beside(vh, vh), NT)
                                      + dot(cat[rows, :VD], vl, NT))
        return 0

    lax.fori_loop(0, H, weight_grads, 0, unroll=True)
    before.point(3)

    def attend(h, _):
        phi = aq[h] * bq[h]
        before.ready(h)
        denom = den[h] + jnp.sum(phi * sums_of(pf, h), axis=1, keepdims=True)
        inv = 1.0 / denom
        den[h] = inv
        out = (num[h] + by_state(phi, state_of(pf, h))) * inv
        att[h] = out.astype(BF16)
        upstream = up[h]
        cat = beside(*split(upstream * inv))
        gcat[h] = cat
        dg = -jnp.sum(upstream * out, axis=1, keepdims=True) * inv
        dgr[h] = dg
        put_state(b_own, h, to_state(phi, cat), jnp.sum(phi * dg, axis=0, keepdims=True))
        after.swap(h).start()
        return 0

    lax.fori_loop(0, H, attend, 0, unroll=True)

    def m_copy(r):
        return remote(m_send.at[r], m_recv.at[r], (m_sem.at[r, 0], m_sem.at[r, 1]),
                      {"head": flip_all(h_me, r & -r)})

    def m_take(b):
        for r in range(0, n_head, 2 * b):
            m_copy(r + b).wait_recv()
            m_own[r // 2] = m_own[r // 2] + m_recv[r + b].astype(F32)
        for r in range(2 * b, n_head, 4 * b):
            m_send[r] = m_own[r // 2].astype(BF16)
            m_copy(r).start()

    order = sorted(range(n_head), reverse=True)
    mixing = []
    for r in order:
        first = pl.multiple_of(flip_all(h_me, r) * TS, TS)
        mixing.append(beside(*[att[h, pl.ds(first, TS), :] for h in range(H)]))
    mixing = jnp.concatenate(mixing, axis=0)
    step = math.gcd(D, 512)
    for c in range(0, D, step):
        part = dot(mixing, w_ref[:, c : c + step], NN)
        for i, r in enumerate(order):
            piece = part[i * TS : (i + 1) * TS]
            if r % 2:
                m_send[r, :, c : c + step] = piece.astype(BF16)
            else:
                m_own[r // 2, :, c : c + step] = piece
    for r in order:
        if r % 2:
            m_copy(r).start()

    after.point(0)
    gcon[0:T, 0 : 2 * LANES] = jnp.zeros((T, 2 * LANES), F32)

    def query_grads(h, _):
        cat = gcat[h]
        dg = dgr[h]
        mask = mask_ref[h, 0:1, :]
        gcon[0:T, 0:HK] = gcon[0:T, 0:HK] + pull(
            on_features(cat, state_of(pf, h), dg * sums_of(pf, h)), h, aq, bq)
        for i in blocks:
            rows, width = slice(i * TB, (i + 1) * TB), (i + 1) * TB
            dw = draw[h, rows, 0:width] * den[h, rows, :] + dg[rows]
            ds = (dw * dsim[h, rows, 0:width]).astype(BF16)
            ds_buf[rows, 0:width] = ds
            gcon[rows, 0:HK] = gcon[rows, 0:HK] + fold(dot(ds, k3[0:width, : 2 * HK], NN)) * mask
        for j in blocks:
            cols = slice(j * TB, (j + 1) * TB)
            gcon[cols, LANES : LANES + HK] = gcon[cols, LANES : LANES + HK] + fold(
                dot(ds_buf[j * TB : T, cols], q2[j * TB : T, :], TN)) * mask
        return 0

    def value_local(h, _):
        for j in blocks:
            cols = slice(j * TB, (j + 1) * TB)
            gvs[h, cols, :] = fold(dot(wh[h, j * TB : T, cols], gcat[h, j * TB : T, :], TN))
        return 0

    head_bits = [1 << i for i in range(n_head.bit_length() - 1)]
    lax.fori_loop(0, H // 4, query_grads, 0, unroll=True)
    m_take(head_bits[0])
    lax.fori_loop(H // 4, H // 2, query_grads, 0, unroll=True)
    after.point(1)
    lax.fori_loop(H // 2, H, query_grads, 0, unroll=True)
    after.point(2)
    lax.fori_loop(0, H, value_local, 0, unroll=True)
    after.point(3)

    def key_grads(h, _):
        after.ready(h)
        dphi = on_features(vcat[h], state_of(pb, h), sums_of(pb, h))
        gcon[0:T, LANES : LANES + HK] = gcon[0:T, LANES : LANES + HK] + pull(dphi, h, ak, bk)
        gvs[h] = gvs[h] + by_state(ak[h] * bk[h], state_of(pb, h))
        return 0

    lax.fori_loop(0, H, key_grads, 0, unroll=True)
    for h in range(H):
        gcon[0:T, (2 + h) * LANES : (3 + h) * LANES] = gvs[h]

    tail = remote(gcon.at[pl.ds(0, RIM)], tail_buf,
                  (halo_sem.at[1, 0], halo_sem.at[1, 1]), {"seq": prv})
    tail.start()

    grads = gcon[0:T, :]
    tr_own[...] = jnp.concatenate(
        [jnp.sum(grads * ext[RIM - j : RIM - j + T, :], axis=0, keepdims=True) for j in range(3)]
        + [jnp.zeros((5, CW), F32)], axis=0)

    def t_copy(d, at):
        return remote(tr_own, tr.at[at], (t_send.at[d], t_recv.at[at]), {"seq": (s + d) % n_seq})

    def t_start(d, _):
        t_copy(d, s).start()
        return 0

    lax.fori_loop(1, n_seq, t_start, 0)
    tr[s] = tr_own[...]

    for b in head_bits[1:]:
        m_take(b)
    mixed_ref[...] = m_own[0].astype(BF16)

    tail.wait_recv()
    tail_ref[...] = jnp.where(s == n_seq - 1, 0.0, tail_buf[...])

    def t_wait(d, _):
        t_copy(d, (s + n_seq - d) % n_seq).wait_recv()
        return 0

    lax.fori_loop(1, n_seq, t_wait, 0)
    taps_ref[...] = lax.fori_loop(1, n_seq, lambda j, acc: acc + tr[j], tr[0])

    halo.wait_send()
    tail.wait_send()
    for _, copy in og_copies.values():
        copy.wait_send()
    for r in range(1, n_head):
        m_copy(r).wait_send()

    def t_drain(d, _):
        t_copy(d, s).wait_send()
        return 0

    lax.fori_loop(1, n_seq, t_drain, 0)
    before.drain()
    after.drain()


def solution(mesh):
    n_seq, n_head = mesh.shape["seq"], mesh.shape["head"]

    def body(query_in, key_in, value_in, conv_query, conv_key, conv_value, out_proj, out_grad):
        T, HK = query_in.shape
        VC = value_in.shape[1]
        D = out_proj.shape[1]
        H = VC // VD
        fk = HK // H
        pick, rows, mask, mask3, feat = feature_tables(fk, H)
        FL = rows.shape[1]
        FP = round_up(feat + FL // LANES, 16)
        CW = 2 * LANES + VC
        TS = T // n_head
        vmem = pl.BlockSpec(memory_space=pltpu.VMEM)
        shape = jax.ShapeDtypeStruct
        big = pltpu.VMEM
        dma = pltpu.SemaphoreType.DMA
        state, half = big((H, 2, FP // 2, VD), F32), big((H, FP // 2, VD), F32)
        mixed, gcon, tail, tap_sums = pl.pallas_call(
            functools.partial(kernel, n_seq, n_head, fk, feat, FP),
            out_shape=(shape((TS, D), BF16), shape((T, CW), F32), shape((RIM, CW), F32), shape((8, CW), F32)),
            in_specs=[vmem] * 6 + [pl.BlockSpec(memory_space=pl.ANY)] + [vmem] * 5,
            out_specs=tuple([vmem] * 4),
            scratch_shapes=[
                big((RIM + T, CW), F32), big((RIM, CW), F32), big((RIM, CW), F32),
                big((T, 3 * HK), BF16), big((T, 3 * HK), BF16), big((T, 2 * HK), BF16),
                big((H, T, 2 * VD), BF16),
                big((H, T, FL), F32), big((H, T, FL), F32), big((H, T, FL), F32), big((H, T, FL), F32),
                big((H, T, T), F32), big((H, T, T), F32), big((H, T, T), BF16), big((T, T), BF16),
                big((H, T, VD), F32), big((H, T, 1), F32), big((H, T, VD), F32),
                big((H, T, 2 * VD), BF16), big((H, T, 1), F32), big((H, T, VD), BF16),
                big((H, T, VD), F32),
                big((n_head, TS, D), BF16), big((n_head, TS, D), BF16),
                big((n_head, TS, D), BF16), big((n_head // 2, TS, D), F32),
                *[state, half, half, half, half, state] * 2,
                big((n_seq, 8, CW), F32), big((8, CW), F32), big((8, CW), F32), big((VC, D), BF16),
                dma((2, 2)), dma((n_head, 2)), dma((n_head, 2)),
                dma((3, H, 2)), dma((3, H, 2)), dma((n_seq,)), dma((n_seq,)), pltpu.SemaphoreType.DMA(()),
            ],
            compiler_params=pltpu.CompilerParams(
                collective_id=0, has_side_effects=True, vmem_limit_bytes=58 * 1024 * 1024),
        )(query_in.T, key_in.T, value_in, conv_query, conv_key, conv_value, out_proj, out_grad,
          jnp.asarray(pick), jnp.asarray(rows), jnp.asarray(mask), jnp.asarray(mask3))
        mixed, gq, gk, gv, gcq, gck, gcv = pl.pallas_call(
            finish,
            out_shape=(
                shape((TS, D), BF16), shape((HK, T), F32), shape((HK, T), F32), shape((T, VC), F32),
                shape((3, HK), F32), shape((3, HK), F32), shape((3, VC), F32),
            ),
            in_specs=[vmem] * 7,
            out_specs=tuple([vmem] * 7),
            compiler_params=pltpu.CompilerParams(vmem_limit_bytes=58 * 1024 * 1024),
        )(conv_query, conv_key, conv_value, mixed, gcon, tail, tap_sums)
        return mixed, gq.T, gk.T, gv, gcq, gck, gcv

    in_specs = (
        P("seq", "head"), P("seq", "head"), P("seq", "head"),
        P(None, "head"), P(None, "head"), P(None, "head"),
        P("head", None), P(("seq", "head"), None),
    )
    out_specs = (
        P(("seq", "head"), None), P("seq", "head"), P("seq", "head"), P("seq", "head"),
        P(None, "head"), P(None, "head"), P(None, "head"),
    )
    return jax.shard_map(body, mesh=mesh, in_specs=in_specs, out_specs=out_specs, check_vma=False)
```
